128 devices in a mesh: depth: 2 (over core), row: 2 (over x_hi), col: 32 (over z, y, x_lo).
Axes of the slice: x: 4 (x_hi: 2, x_lo: 2; x = x_hi * 2 + x_lo), y: 4, z: 4, core: 2. Of those that a mesh axis runs over, the one named last changes fastest.
Arguments:
- tokens_in: bfloat16 [1024, 6144], P(('depth', 'col'), 'row'), may hold values from -6 to 6
- w_in: bfloat16 [6144, 24576], P('row', ('depth', 'col')), may hold values from -0.078125 to 0.078125
- w_out: bfloat16 [24576, 6144], P(('depth', 'col'), 'row'), may hold values from -0.0390625 to 0.0390625
- grad_output: bfloat16 [1024, 6144], P(('depth', 'col'), 'row'), may hold values from -6 to 6
Outputs:
- output: bfloat16 [1024, 6144], P(('depth', 'col'), 'row')
- grad_input: bfloat16 [1024, 6144], P(('depth', 'col'), 'row')
- grad_w_in: float32 [6144, 24576], P('row', ('depth', 'col'))
- grad_w_out: float32 [24576, 6144], P(('depth', 'col'), 'row')
The draws below stay inside these ranges and needn't reach their ends.
All inputs are finite; a program needn't handle non-finite values.
Results may differ from the reference program's by a relative error of at most 0.005.
Values may be sent and summed in bfloat16 or wider, within the bound.
A program may use at most 128 MiB of HBM per device.

```python
import jax
import jax.numpy as jnp

D = 6144
FF = 24576
TOKENS = 1024


def steps_of(rng, shape, pieces, least, top_value):
    def one(position, parts):
        steps = jax.random.uniform(jax.random.fold_in(jax.random.fold_in(rng, 6), position), (parts,), jnp.float32, least / len(pieces), top_value / len(pieces))
        return jnp.repeat(jnp.exp(steps), shape[position] // parts).reshape((-1,) + (1,) * (len(shape) - position - 1))

    level = one(*pieces[0])
    for cut in pieces[1:]:
        level = level * one(*cut)
    return level


def gaussian(stream_key, extent, spread, bound, pieces=(), held_as=jnp.bfloat16):
    loudness = steps_of(stream_key, extent, pieces, -0.22, 0.18) if pieces else 1.0
    drawn = jax.random.normal(stream_key, extent, jnp.float32) * spread * loudness
    return jnp.minimum(jnp.maximum(drawn, -bound), bound).astype(held_as)


def setup_inputs(seed: int = 0) -> dict:
    seeds = jax.random.split(jax.random.key(seed), 5)
    return {
        "tokens_in": gaussian(seeds[0], (TOKENS, D), 1.0, 6.0, ((0, 64), (1, 2))),
        "w_in": gaussian(seeds[1], (D, FF), D ** -0.5, 0.078125, ((0, 2), (1, 64))),
        "w_out": gaussian(seeds[2], (FF, D), FF ** -0.5, 0.0390625, ((0, 64), (1, 2))),
        "grad_output": gaussian(seeds[3], (TOKENS, D), 1.0, 6.0, ((0, 64), (1, 2))),
    }


def gelu_value(hidden):
    inner = 0.7978845608 * (hidden + 0.044715 * hidden * hidden * hidden)
    return 0.5 * hidden * (1.0 + jnp.tanh(inner))


def gelu_slope(hidden):
    inner = 0.7978845608 * (hidden + 0.044715 * hidden * hidden * hidden)
    tangent = jnp.tanh(inner)
    return 0.5 * (1.0 + tangent) + 0.5 * hidden * (1.0 - tangent * tangent) * 0.7978845608 * (1.0 + 3.0 * 0.044715 * hidden * hidden)


def reference(tokens_in, w_in, w_out, grad_output):
    pre_act = jnp.dot(tokens_in, w_in, preferred_element_type=jnp.float32)
    d_act = jnp.dot(grad_output, w_out.T, preferred_element_type=jnp.float32)
    act = gelu_value(pre_act).astype(jnp.bfloat16)
    output = jnp.dot(act, w_out, preferred_element_type=jnp.float32).astype(jnp.bfloat16)
    d_pre = (d_act * gelu_slope(pre_act)).astype(jnp.bfloat16)
    grad_w_out = jnp.dot(act.T, grad_output, preferred_element_type=jnp.float32)
    grad_w_in = jnp.dot(tokens_in.T, d_pre, preferred_element_type=jnp.float32)
    grad_input = jnp.dot(d_pre, w_in.T, preferred_element_type=jnp.float32).astype(jnp.bfloat16)
    return output, grad_input, grad_w_in, grad_w_out
```

```python
import functools

import jax
import jax.numpy as jnp
from jax import lax
from jax.experimental import pallas as pl
from jax.experimental.pallas import tpu as pltpu
from jax.sharding import PartitionSpec as P

MESH = pl.DeviceIdType.MESH
BF16, F32 = jnp.bfloat16, jnp.float32
OFFSETS = (0, 1, 3, 2)
N_REMOTE = 128
N_LOCAL = 16


def contract_rows(left, right):
    return lax.dot_general(left, right, (((0,), (0,)), ((), ())), preferred_element_type=F32)


def nn(left, right):
    return jnp.dot(left, right, preferred_element_type=F32)


def nt(left, right):
    return lax.dot_general(left, right, (((1,), (1,)), ((), ())), preferred_element_type=F32)


def kernel(
    tokens, w_in, w_out, cotangent,
    out, gin, tokens_every, cotangent_every, act_every, dpre_every,
    g_tok, g_cot, wi, wo, pre, dact, s_pre, r_pre, s_dact, r_dact, act, dpre,
    q2, r2, mid, s1, r1, acc, u2, v2, fin, s3, r3,
    send, recv, local,
):
    rows, feat = tokens.shape
    hid = w_in.shape[1]
    slab = 4 * rows
    depth, row, col = lax.axis_index("depth"), lax.axis_index("row"), lax.axis_index("col")
    low = lax.rem(col, 2)
    y = lax.rem(lax.div(col, 2), 4)
    z = lax.div(col, 8)

    def at(dy=0, dz=0, lo=None, r=None, d=None):
        c = lax.rem(z + dz, 4) * 8 + lax.rem(y + dy, 4) * 2 + (low if lo is None else lo)
        return (depth if d is None else d, row if r is None else r, c)

    x_partner = at(lo=1 - low)
    row_partner = at(r=1 - row)
    core_partner = at(d=1 - depth)
    along_y = {o: at(dy=o) for o in (1, 2, 3)}
    along_z = {o: at(dz=o) for o in (1, 2, 3)}
    ring1 = (along_z, along_y)
    ring2 = (along_y, along_z)
    own = (y, z)
    sub = (z, y)

    counter, counter_local, sent = [0], [0], []

    def remote(src, dst, device):
        i = counter[0]
        counter[0] += 1
        copy = pltpu.make_async_remote_copy(
            src_ref=src, dst_ref=dst, send_sem=send.at[i], recv_sem=recv.at[i],
            device_id=device, device_id_type=MESH,
        )
        copy.start()
        sent.append(copy)
        return copy

    def here(src, dst):
        i = counter_local[0]
        counter_local[0] += 1
        copy = pltpu.make_async_copy(src, dst, local.at[i])
        copy.start()
        return copy

    def piece(j):
        return pl.ds(pl.multiple_of(j * rows, rows), rows)

    def ring_at(h, o):
        return lax.rem(own[h] + o, 4)

    my_i = y + low * (z - y)
    my_j = z + low * (y - z)
    own_copies = [
        here(tokens, g_tok.at[low, my_i, piece(my_j)]),
        here(cotangent, g_cot.at[low, my_i, piece(my_j)]),
    ]
    weight_copies = [
        here(w_in, wi.at[:, pl.ds(0, hid)]),
        here(w_out, wo.at[pl.ds(0, hid)]),
    ]

    barrier = pltpu.get_barrier_semaphore()
    friends = [x_partner, row_partner, core_partner] + list(along_y.values()) + list(along_z.values())
    for friend in friends:
        pl.semaphore_signal(barrier, inc=1, device_id=friend, device_id_type=MESH)
    pl.semaphore_wait(barrier, len(friends))

    gathered = (g_tok, g_cot)
    g0 = [
        remote(src, g.at[low, my_i, piece(my_j)], x_partner)
        for src, g in ((tokens, g_tok), (cotangent, g_cot))
    ]
    weight_in = remote(w_in, wi.at[:, pl.ds(hid, hid)], core_partner)
    weight_out = remote(w_out, wo.at[pl.ds(hid, hid)], core_partner)

    def gather_one(g):
        copies = []
        for h in range(2):
            block = g.at[h, own[h], piece(sub[h])]
            copies += [remote(block, block, ring1[h][o]) for o in (1, 3, 2)]
        return copies

    def half(k):
        return pl.ds(k * 2 * rows, 2 * rows)

    def gather_two(g):
        first, second = [], []
        for h in range(2):
            for o, order in ((1, (0, 1)), (3, (1, 0))):
                part = [g.at[h, own[h], half(k)] for k in order]
                first.append(remote(part[0], part[0], ring2[h][o]))
        for h in range(2):
            for o, order in ((1, (0, 1)), (3, (1, 0))):
                part = g.at[h, own[h], half(order[1])]
                second.append(remote(part, part, ring2[h][o]))
        return first, second

    def gather_three(g):
        copies = []
        for h in range(2):
            left = g.at[h, ring_at(h, 3), half(0)]
            copies.append(remote(left, left, ring2[h][1]))
            right = g.at[h, ring_at(h, 1), half(1)]
            copies.append(remote(right, right, ring2[h][3]))
        return copies

    def arrived(copies):
        for copy in copies:
            copy.wait_recv()

    g1 = []
    for k in range(2):
        own_copies[k].wait()
        g0[k].wait_recv()
        g1.append(gather_one(gathered[k]))
    arrived(g1[0])
    x2 = gather_two(g_tok)

    tile = 256
    n_hid = 2 * hid // tile

    def rows_of(g, o):
        return jnp.concatenate([g[h, ring_at(h, o)] for h in range(2)], axis=0)

    def pre_step(s):
        chunk = rows_of(g_tok, OFFSETS[s])

        def body(t, _):
            cols = pl.ds(pl.multiple_of(t * tile, tile), tile)
            value = nn(chunk, wi[:, cols])
            pre[s, :, cols] = value
            s_pre[s, :, cols] = value.astype(BF16)
            return 0

        lax.fori_loop(0, n_hid, body, 0)
        return remote(s_pre.at[s], r_pre.at[s], row_partner)

    def dact_step(s):
        chunk = rows_of(g_cot, OFFSETS[s])

        def body(t, _):
            cols = pl.ds(pl.multiple_of(t * tile, tile), tile)
            value = nt(chunk, wo[cols, :])
            dact[s, :, cols] = value
            s_dact[s, :, cols] = value.astype(BF16)
            return 0

        lax.fori_loop(0, n_hid, body, 0)
        return remote(s_dact.at[s], r_dact.at[s], row_partner)

    def act_step(s, copy):
        copy.wait_recv()
        for h in range(2):
            i = ring_at(h, OFFSETS[s])

            def body(t, _):
                r_in = pl.ds(pl.multiple_of(h * slab + t * 16, 16), 16)
                r_out = pl.ds(pl.multiple_of(t * 16, 16), 16)
                hidden = pre[s, r_in, :] + r_pre[s, r_in, :].astype(F32)
                square = hidden * hidden
                inner = 0.7978845608 * (hidden + 0.044715 * square * hidden)
                tangent = jnp.tanh(inner)
                act[h, i, r_out, :] = (0.5 * hidden * (1.0 + tangent)).astype(BF16)
                pre[s, r_in, :] = 0.5 * (1.0 + tangent) + 0.5 * hidden * (
                    1.0 - tangent * tangent
                ) * 0.7978845608 * (1.0 + 3.0 * 0.044715 * square)
                return 0

            lax.fori_loop(0, slab // 16, body, 0)

    def dpre_step(s, copy):
        copy.wait_recv()
        for h in range(2):
            i = ring_at(h, OFFSETS[s])

            def body(t, _):
                r_in = pl.ds(pl.multiple_of(h * slab + t * 16, 16), 16)
                r_out = pl.ds(pl.multiple_of(t * 16, 16), 16)
                total = dact[s, r_in, :] + r_dact[s, r_in, :].astype(F32)
                dpre[h, i, r_out, :] = (total * pre[s, r_in, :]).astype(BF16)
                return 0

            lax.fori_loop(0, slab // 16, body, 0)

    wide = 512
    n_wide = feat // wide
    low_rows, high_rows = slice(0, 2 * rows), slice(2 * rows, 4 * rows)

    def project(k, s):
        chunk = rows_of((act, dpre)[k], OFFSETS[s])
        o = OFFSETS[s]

        def body(t, _):
            cols = pl.ds(pl.multiple_of(t * wide, wide), wide)
            value = nn(chunk, wo[:, cols]) if k == 0 else nt(chunk, wi[cols, :])
            for h in range(2):
                part = value[h * slab:(h + 1) * slab]
                if o == 2:
                    q2[k, h, :, cols] = part.astype(BF16)
                elif o == 1:
                    s1[k, h, 0, high_rows, cols] = part[high_rows].astype(BF16)
                    mid[k, h, 0, :, cols] = part[low_rows]
                elif o == 3:
                    s1[k, h, 1, low_rows, cols] = part[low_rows].astype(BF16)
                    mid[k, h, 1, :, cols] = part[high_rows]
                else:
                    acc[k, h, :, cols] = part
            return 0

        lax.fori_loop(0, n_wide, body, 0)

    def scatter_far(k):
        copies = []
        for h in range(2):
            copies.append(remote(q2.at[k, h, low_rows], r2.at[k, h, 0], ring2[h][1]))
            copies.append(remote(q2.at[k, h, high_rows], r2.at[k, h, 1], ring2[h][3]))
        return copies

    def scatter_near(k, side):
        part = (high_rows, low_rows)[side]
        return [
            remote(s1.at[k, h, side, part], r1.at[k, h, side, part], ring2[h][(1, 3)[side]])
            for h in range(2)
        ]

    def scatter_merge(k, far):
        copies = []
        for h in range(2):
            for side in range(2):
                far[2 * h + side].wait_recv()
                base = side * 2 * rows

                def body(t, _):
                    r_in = pl.ds(pl.multiple_of(t * 16, 16), 16)
                    r_out = pl.ds(pl.multiple_of(base + t * 16, 16), 16)
                    total = mid[k, h, side, r_in, :] + r2[k, h, side, r_in, :].astype(F32)
                    s1[k, h, side, r_out, :] = total.astype(BF16)
                    return 0

                lax.fori_loop(0, 2 * rows // 16, body, 0)
                part = (low_rows, high_rows)[side]
                copies.append(
                    remote(s1.at[k, h, side, part], r1.at[k, h, side, part], ring2[h][(1, 3)[side]])
                )
        return copies

    def scatter_two(k, near, merged):
        arrived(near)
        arrived(merged)
        copies = []
        for h in range(2):
            for slot, o in enumerate((1, 3, 2)):
                r_in = piece(lax.rem(sub[h] + o, 4))
                total = acc[k, h, r_in, :] + r1[k, h, 0, r_in, :].astype(F32)
                u2[k, h, slot] = (total + r1[k, h, 1, r_in, :].astype(F32)).astype(BF16)
                copies.append(remote(u2.at[k, h, slot], v2.at[k, h, slot], ring1[h][o]))
        return copies

    def scatter_three(k, copies):
        arrived(copies)
        for h in range(2):
            r_in = piece(sub[h])
            total = acc[k, h, r_in, :] + r1[k, h, 0, r_in, :].astype(F32)
            total += r1[k, h, 1, r_in, :].astype(F32)
            for slot in range(3):
                total += v2[k, h, slot].astype(F32)
            fin[k, h] = total
        s3[k] = fin[k, 1 - low].astype(BF16)
        return remote(s3.at[k], r3.at[k], x_partner)

    def finish(k, copy):
        copy.wait_recv()
        (out, gin)[k][...] = (fin[k, low] + r3[k].astype(F32)).astype(BF16)

    weight_copies[0].wait()
    weight_in.wait_recv()
    p = [pre_step(0)]
    arrived(x2[0])
    x3 = gather_three(g_tok)
    arrived(g1[1])
    c2 = gather_two(g_cot)
    arrived(x2[1])
    p.append(pre_step(1))
    p.append(pre_step(2))
    arrived(x3)
    p.append(pre_step(3))
    every = [here(g_tok, tokens_every.at[0]), remote(g_tok, tokens_every.at[1], core_partner)]
    weight_copies[1].wait()
    weight_out.wait_recv()
    q = [dact_step(0)]
    act_step(0, p[0])
    arrived(c2[0])
    c3 = gather_three(g_cot)
    act_step(1, p[1])
    act_step(2, p[2])
    act_step(3, p[3])
    project(0, 3)
    far0 = scatter_far(0)
    project(0, 1)
    near0 = scatter_near(0, 0)
    project(0, 2)
    near0 += scatter_near(0, 1)
    arrived(c2[1])
    q.append(dact_step(1))
    q.append(dact_step(2))
    arrived(c3)
    q.append(dact_step(3))
    merged0 = scatter_merge(0, far0)
    project(0, 0)
    every += [here(g_cot, cotangent_every.at[0]), remote(g_cot, cotangent_every.at[1], core_partner)]
    mine, other = pl.ds(0, hid), pl.ds(hid, hid)
    every += [
        here(act.at[:, :, :, mine], act_every.at[0]),
        remote(act.at[:, :, :, other], act_every.at[1], core_partner),
    ]
    dpre_step(3, q[3])
    project(1, 3)
    far1 = scatter_far(1)
    dpre_step(1, q[1])
    project(1, 1)
    near1 = scatter_near(1, 0)
    dpre_step(2, q[2])
    project(1, 2)
    near1 += scatter_near(1, 1)
    two0 = scatter_two(0, near0, merged0)
    dpre_step(0, q[0])
    project(1, 0)
    every += [
        here(dpre.at[:, :, :, mine], dpre_every.at[0]),
        remote(dpre.at[:, :, :, other], dpre_every.at[1], core_partner),
    ]
    merged1 = scatter_merge(1, far1)
    three0 = scatter_three(0, two0)
    finish(0, three0)
    two1 = scatter_two(1, near1, merged1)
    three1 = scatter_three(1, two1)
    finish(1, three1)
    for i in range(0, len(every), 2):
        every[i].wait()
        every[i + 1].wait_recv()
    for copy in sent:
        copy.wait_send()


def exchange(tokens_in, w_in, w_out, grad_output):
    rows, feat = tokens_in.shape
    hid = w_in.shape[1]
    slab = 4 * rows
    vmem, hbm = pl.BlockSpec(memory_space=pltpu.VMEM), pl.BlockSpec(memory_space=pl.ANY)
    shape = jax.ShapeDtypeStruct
    scratch = [
        ((2, 4, slab, feat), BF16),
        ((2, 4, slab, feat), BF16),
        ((feat, 2 * hid), BF16),
        ((2 * hid, feat), BF16),
        ((4, 2 * slab, 2 * hid), F32),
        ((4, 2 * slab, 2 * hid), F32),
        ((4, 2 * slab, 2 * hid), BF16),
        ((4, 2 * slab, 2 * hid), BF16),
        ((4, 2 * slab, 2 * hid), BF16),
        ((4, 2 * slab, 2 * hid), BF16),
        ((2, 4, slab, 2 * hid), BF16),
        ((2, 4, slab, 2 * hid), BF16),
        ((2, 2, slab, feat), BF16),
        ((2, 2, 2, 2 * rows, feat), BF16),
        ((2, 2, 2, 2 * rows, feat), F32),
        ((2, 2, 2, slab, feat), BF16),
        ((2, 2, 2, slab, feat), BF16),
        ((2, 2, slab, feat), F32),
        ((2, 2, 3, rows, feat), BF16),
        ((2, 2, 3, rows, feat), BF16),
        ((2, 2, rows, feat), F32),
        ((2, rows, feat), BF16),
        ((2, rows, feat), BF16),
    ]
    return pl.pallas_call(
        kernel,
        out_shape=[
            shape((rows, feat), BF16),
            shape((rows, feat), BF16),
            shape((2, 2, 4, slab, feat), BF16),
            shape((2, 2, 4, slab, feat), BF16),
            shape((2, 2, 4, slab, hid), BF16),
            shape((2, 2, 4, slab, hid), BF16),
        ],
        in_specs=[hbm] * 4,
        out_specs=[vmem] * 2 + [hbm] * 4,
        scratch_shapes=[pltpu.VMEM(*s) for s in scratch] + [
            pltpu.SemaphoreType.DMA((N_REMOTE,)),
            pltpu.SemaphoreType.DMA((N_REMOTE,)),
            pltpu.SemaphoreType.DMA((N_LOCAL,)),
        ],
        compiler_params=pltpu.CompilerParams(
            collective_id=0, has_side_effects=True, vmem_limit_bytes=60 * 2**20
        ),
        name="exchange",
    )(tokens_in, w_in, w_out, grad_output)


def per_device(tokens_in, w_in, w_out, grad_output):
    feat, hid = w_in.shape
    output, grad_input, tokens_every, cotangent_every, act_owned, dpre_owned = exchange(
        tokens_in, w_in, w_out, grad_output
    )
    grad_w_out = contract_rows(act_owned.reshape(-1, hid), cotangent_every.reshape(-1, feat))
    grad_w_in = contract_rows(tokens_every.reshape(-1, feat), dpre_owned.reshape(-1, hid))
    return (output, grad_input, grad_w_in, grad_w_out)


def solution(mesh):
    placed = (
        P(("depth", "col"), "row"),
        P("row", ("depth", "col")),
        P(("depth", "col"), "row"),
        P(("depth", "col"), "row"),
    )
    return jax.shard_map(
        per_device,
        mesh=mesh,
        in_specs=placed,
        out_specs=(
            P(("depth", "col"), "row"),
            P(("depth", "col"), "row"),
            P("row", ("depth", "col")),
            P(("depth", "col"), "row"),
        ),
        check_vma=False,
    )
```

```python
import functools

import jax
import jax.numpy as jnp
from jax import lax
from jax.experimental import pallas as pl
from jax.experimental.pallas import tpu as pltpu
from jax.sharding import PartitionSpec as P

MESH = pl.DeviceIdType.MESH
BF16, F32 = jnp.bfloat16, jnp.float32
OFFSETS = (0, 1, 3, 2)
N_REMOTE = 128
N_LOCAL = 16


def contract_rows(left, right):
    return lax.dot_general(left, right, (((0,), (0,)), ((), ())), preferred_element_type=F32)


def nn(left, right):
    return jnp.dot(left, right, preferred_element_type=F32)


def nt(left, right):
    return lax.dot_general(left, right, (((1,), (1,)), ((), ())), preferred_element_type=F32)


def kernel(
    tokens, w_in, w_out, cotangent,
    out, gin, grad_in, grad_out,
    g_tok, g_cot, e_tok, e_cot, e_act, e_dpre, act_t, wi, wo, pre, dact, s_pre, r_pre, s_dact, r_dact, act, dpre,
    q2, r2, mid, s1, r1, acc, u2, v2, fin, s3, r3,
    send, recv, local,
):
    rows, feat = tokens.shape
    hid = w_in.shape[1]
    slab = 4 * rows
    depth, row, col = lax.axis_index("depth"), lax.axis_index("row"), lax.axis_index("col")
    low = lax.rem(col, 2)
    y = lax.rem(lax.div(col, 2), 4)
    z = lax.div(col, 8)

    def at(dy=0, dz=0, lo=None, r=None, d=None):
        c = lax.rem(z + dz, 4) * 8 + lax.rem(y + dy, 4) * 2 + (low if lo is None else lo)
        return (depth if d is None else d, row if r is None else r, c)

    x_partner = at(lo=1 - low)
    row_partner = at(r=1 - row)
    core_partner = at(d=1 - depth)
    along_y = {o: at(dy=o) for o in (1, 2, 3)}
    along_z = {o: at(dz=o) for o in (1, 2, 3)}
    ring1 = (along_z, along_y)
    ring2 = (along_y, along_z)
    own = (y, z)
    sub = (z, y)

    counter, counter_local, sent = [0], [0], []

    def remote(src, dst, device):
        i = counter[0]
        counter[0] += 1
        copy = pltpu.make_async_remote_copy(
            src_ref=src, dst_ref=dst, send_sem=send.at[i], recv_sem=recv.at[i],
            device_id=device, device_id_type=MESH,
        )
        copy.start()
        sent.append(copy)
        return copy

    def here(src, dst):
        i = counter_local[0]
        counter_local[0] += 1
        copy = pltpu.make_async_copy(src, dst, local.at[i])
        copy.start()
        return copy

    def piece(j):
        return pl.ds(pl.multiple_of(j * rows, rows), rows)

    def ring_at(h, o):
        return lax.rem(own[h] + o, 4)

    my_i = y + low * (z - y)
    my_j = z + low * (y - z)
    own_copies = [
        here(tokens, g_tok.at[low, my_i, piece(my_j)]),
        here(cotangent, g_cot.at[low, my_i, piece(my_j)]),
    ]
    weight_copies = [
        here(w_in, wi.at[:, pl.ds(0, hid)]),
        here(w_out, wo.at[pl.ds(0, hid)]),
    ]

    barrier = pltpu.get_barrier_semaphore()
    friends = [x_partner, row_partner, core_partner] + list(along_y.values()) + list(along_z.values())
    for friend in friends:
        pl.semaphore_signal(barrier, inc=1, device_id=friend, device_id_type=MESH)
    pl.semaphore_wait(barrier, len(friends))

    gathered = (g_tok, g_cot)
    g0 = [
        remote(src, g.at[low, my_i, piece(my_j)], x_partner)
        for src, g in ((tokens, g_tok), (cotangent, g_cot))
    ]
    weight_in = remote(w_in, wi.at[:, pl.ds(hid, hid)], core_partner)
    weight_out = remote(w_out, wo.at[pl.ds(hid, hid)], core_partner)

    def gather_one(g):
        copies = []
        for h in range(2):
            block = g.at[h, own[h], piece(sub[h])]
            copies += [remote(block, block, ring1[h][o]) for o in (1, 3, 2)]
        return copies

    def half(k):
        return pl.ds(k * 2 * rows, 2 * rows)

    def gather_two(g):
        first, second = [], []
        for h in range(2):
            for o, order in ((1, (0, 1)), (3, (1, 0))):
                part = [g.at[h, own[h], half(k)] for k in order]
                first.append(remote(part[0], part[0], ring2[h][o]))
        for h in range(2):
            for o, order in ((1, (0, 1)), (3, (1, 0))):
                part = g.at[h, own[h], half(order[1])]
                second.append(remote(part, part, ring2[h][o]))
        return first, second

    def gather_three(g):
        copies = []
        for h in range(2):
            left = g.at[h, ring_at(h, 3), half(0)]
            copies.append(remote(left, left, ring2[h][1]))
            right = g.at[h, ring_at(h, 1), half(1)]
            copies.append(remote(right, right, ring2[h][3]))
        return copies

    def arrived(copies):
        for copy in copies:
            copy.wait_recv()

    g1 = []
    for k in range(2):
        own_copies[k].wait()
        g0[k].wait_recv()
        g1.append(gather_one(gathered[k]))
    arrived(g1[0])
    x2 = gather_two(g_tok)

    tile = 256
    n_hid = 2 * hid // tile

    def rows_of(g, o):
        return jnp.concatenate([g[h, ring_at(h, o)] for h in range(2)], axis=0)

    def pre_step(s):
        chunk = rows_of(g_tok, OFFSETS[s])

        def body(t, _):
            cols = pl.ds(pl.multiple_of(t * tile, tile), tile)
            value = nn(chunk, wi[:, cols])
            pre[s, :, cols] = value
            s_pre[s, :, cols] = value.astype(BF16)
            return 0

        lax.fori_loop(0, n_hid, body, 0)
        return remote(s_pre.at[s], r_pre.at[s], row_partner)

    def dact_step(s):
        chunk = rows_of(g_cot, OFFSETS[s])

        def body(t, _):
            cols = pl.ds(pl.multiple_of(t * tile, tile), tile)
            value = nt(chunk, wo[cols, :])
            dact[s, :, cols] = value
            s_dact[s, :, cols] = value.astype(BF16)
            return 0

        lax.fori_loop(0, n_hid, body, 0)
        return remote(s_dact.at[s], r_dact.at[s], row_partner)

    def act_step(s, copy):
        copy.wait_recv()
        for h in range(2):
            i = ring_at(h, OFFSETS[s])

            def body(t, _):
                r_in = pl.ds(pl.multiple_of(h * slab + t * 16, 16), 16)
                r_out = pl.ds(pl.multiple_of(t * 16, 16), 16)
                hidden = pre[s, r_in, :] + r_pre[s, r_in, :].astype(F32)
                square = hidden * hidden
                inner = 0.7978845608 * (hidden + 0.044715 * square * hidden)
                tangent = jnp.tanh(inner)
                act[h, i, r_out, :] = (0.5 * hidden * (1.0 + tangent)).astype(BF16)
                pre[s, r_in, :] = 0.5 * (1.0 + tangent) + 0.5 * hidden * (
                    1.0 - tangent * tangent
                ) * 0.7978845608 * (1.0 + 3.0 * 0.044715 * square)
                return 0

            lax.fori_loop(0, slab // 16, body, 0)

    def dpre_step(s, copy):
        copy.wait_recv()
        for h in range(2):
            i = ring_at(h, OFFSETS[s])

            def body(t, _):
                r_in = pl.ds(pl.multiple_of(h * slab + t * 16, 16), 16)
                r_out = pl.ds(pl.multiple_of(t * 16, 16), 16)
                total = dact[s, r_in, :] + r_dact[s, r_in, :].astype(F32)
                dpre[h, i, r_out, :] = (total * pre[s, r_in, :]).astype(BF16)
                return 0

            lax.fori_loop(0, slab // 16, body, 0)

    wide = 512
    n_wide = feat // wide
    low_rows, high_rows = slice(0, 2 * rows), slice(2 * rows, 4 * rows)

    def project(k, s):
        chunk = rows_of((act, dpre)[k], OFFSETS[s])
        o = OFFSETS[s]

        def body(t, _):
            cols = pl.ds(pl.multiple_of(t * wide, wide), wide)
            value = nn(chunk, wo[:, cols]) if k == 0 else nt(chunk, wi[cols, :])
            for h in range(2):
                part = value[h * slab:(h + 1) * slab]
                if o == 2:
                    q2[k, h, :, cols] = part.astype(BF16)
                elif o == 1:
                    s1[k, h, 0, high_rows, cols] = part[high_rows].astype(BF16)
                    mid[k, h, 0, :, cols] = part[low_rows]
                elif o == 3:
                    s1[k, h, 1, low_rows, cols] = part[low_rows].astype(BF16)
                    mid[k, h, 1, :, cols] = part[high_rows]
                else:
                    acc[k, h, :, cols] = part
            return 0

        lax.fori_loop(0, n_wide, body, 0)

    def scatter_far(k):
        copies = []
        for h in range(2):
            copies.append(remote(q2.at[k, h, low_rows], r2.at[k, h, 0], ring2[h][1]))
            copies.append(remote(q2.at[k, h, high_rows], r2.at[k, h, 1], ring2[h][3]))
        return copies

    def scatter_near(k, side):
        part = (high_rows, low_rows)[side]
        return [
            remote(s1.at[k, h, side, part], r1.at[k, h, side, part], ring2[h][(1, 3)[side]])
            for h in range(2)
        ]

    def scatter_merge(k, far):
        copies = []
        for h in range(2):
            for side in range(2):
                far[2 * h + side].wait_recv()
                base = side * 2 * rows

                def body(t, _):
                    r_in = pl.ds(pl.multiple_of(t * 16, 16), 16)
                    r_out = pl.ds(pl.multiple_of(base + t * 16, 16), 16)
                    total = mid[k, h, side, r_in, :] + r2[k, h, side, r_in, :].astype(F32)
                    s1[k, h, side, r_out, :] = total.astype(BF16)
                    return 0

                lax.fori_loop(0, 2 * rows // 16, body, 0)
                part = (low_rows, high_rows)[side]
                copies.append(
                    remote(s1.at[k, h, side, part], r1.at[k, h, side, part], ring2[h][(1, 3)[side]])
                )
        return copies

    def scatter_two(k, near, merged):
        arrived(near)
        arrived(merged)
        copies = []
        for h in range(2):
            for slot, o in enumerate((1, 3, 2)):
                r_in = piece(lax.rem(sub[h] + o, 4))
                total = acc[k, h, r_in, :] + r1[k, h, 0, r_in, :].astype(F32)
                u2[k, h, slot] = (total + r1[k, h, 1, r_in, :].astype(F32)).astype(BF16)
                copies.append(remote(u2.at[k, h, slot], v2.at[k, h, slot], ring1[h][o]))
        return copies

    def scatter_three(k, copies):
        arrived(copies)
        for h in range(2):
            r_in = piece(sub[h])
            total = acc[k, h, r_in, :] + r1[k, h, 0, r_in, :].astype(F32)
            total += r1[k, h, 1, r_in, :].astype(F32)
            for slot in range(3):
                total += v2[k, h, slot].astype(F32)
            fin[k, h] = total
        s3[k] = fin[k, 1 - low].astype(BF16)
        return remote(s3.at[k], r3.at[k], x_partner)

    def finish(k, copy):
        copy.wait_recv()
        (out, gin)[k][...] = (fin[k, low] + r3[k].astype(F32)).astype(BF16)

    mine, other = pl.ds(0, hid), pl.ds(hid, hid)
    tokens_all = 8 * slab

    def flat(value):
        return value.reshape(tokens_all, value.shape[-1])

    def turn_act():
        act_t[0] = jnp.transpose(flat(act[:, :, :, mine]))
        act_t[1] = jnp.transpose(flat(e_act[...]))

    def grad_out_part(start, stop):
        def body(t, _):
            cols = pl.ds(pl.multiple_of(t * tile, tile), tile)
            value = nn(act_t[0], flat(g_cot[:, :, :, cols]))
            grad_out[:, cols] = value + nn(act_t[1], flat(e_cot[:, :, :, cols]))
            return 0

        lax.fori_loop(start, stop, body, 0)

    def grad_in_part(start, stop):
        def body(t, _):
            cols = pl.ds(pl.multiple_of(t * tile, tile), tile)
            value = contract_rows(flat(g_tok[:, :, :, cols]), flat(dpre[:, :, :, mine]))
            value += contract_rows(flat(e_tok[:, :, :, cols]), flat(e_dpre[...]))
            grad_in[cols, :] = value
            return 0

        lax.fori_loop(start, stop, body, 0)

    weight_copies[0].wait()
    weight_in.wait_recv()
    p = [pre_step(0)]
    arrived(x2[0])
    x3 = gather_three(g_tok)
    arrived(g1[1])
    c2 = gather_two(g_cot)
    arrived(x2[1])
    p.append(pre_step(1))
    p.append(pre_step(2))
    arrived(x3)
    p.append(pre_step(3))
    every_tok = remote(g_tok, e_tok, core_partner)
    weight_copies[1].wait()
    weight_out.wait_recv()
    q = [dact_step(0)]
    act_step(0, p[0])
    arrived(c2[0])
    c3 = gather_three(g_cot)
    act_step(1, p[1])
    act_step(2, p[2])
    act_step(3, p[3])
    project(0, 3)
    far0 = scatter_far(0)
    project(0, 1)
    near0 = scatter_near(0, 0)
    project(0, 2)
    near0 += scatter_near(0, 1)
    every_act = remote(act.at[:, :, :, other], e_act, core_partner)
    arrived(c2[1])
    arrived(c3)
    q += [None, None, dact_step(3)]
    q[1] = dact_step(1)
    q[2] = dact_step(2)
    merged0 = scatter_merge(0, far0)
    every_cot = remote(g_cot, e_cot, core_partner)
    dpre_step(3, q[3])
    project(1, 3)
    far1 = scatter_far(1)
    dpre_step(1, q[1])
    project(1, 1)
    near1 = scatter_near(1, 0)
    dpre_step(2, q[2])
    project(1, 2)
    near1 += scatter_near(1, 1)
    project(0, 0)
    two0 = scatter_two(0, near0, merged0)
    dpre_step(0, q[0])
    every_dpre = remote(dpre.at[:, :, :, other], e_dpre, core_partner)
    merged1 = scatter_merge(1, far1)
    project(1, 0)
    every_act.wait_recv()
    turn_act()
    three0 = scatter_three(0, two0)
    every_cot.wait_recv()
    grad_out_part(0, feat // tile)
    finish(0, three0)
    two1 = scatter_two(1, near1, merged1)
    every_tok.wait_recv()
    every_dpre.wait_recv()
    grad_in_part(0, feat // tile // 2)
    three1 = scatter_three(1, two1)
    grad_in_part(feat // tile // 2, feat // tile)
    finish(1, three1)
    for copy in sent:
        copy.wait_send()


def exchange(tokens_in, w_in, w_out, grad_output):
    rows, feat = tokens_in.shape
    hid = w_in.shape[1]
    slab = 4 * rows
    vmem, hbm = pl.BlockSpec(memory_space=pltpu.VMEM), pl.BlockSpec(memory_space=pl.ANY)
    scratch = [
        ((2, 4, slab, feat), BF16),
        ((2, 4, slab, feat), BF16),
        ((2, 4, slab, feat), BF16),
        ((2, 4, slab, feat), BF16),
        ((2, 4, slab, hid), BF16),
        ((2, 4, slab, hid), BF16),
        ((2, hid, 8 * slab), BF16),
        ((feat, 2 * hid), BF16),
        ((2 * hid, feat), BF16),
        ((4, 2 * slab, 2 * hid), F32),
        ((4, 2 * slab, 2 * hid), F32),
        ((4, 2 * slab, 2 * hid), BF16),
        ((4, 2 * slab, 2 * hid), BF16),
        ((4, 2 * slab, 2 * hid), BF16),
        ((4, 2 * slab, 2 * hid), BF16),
        ((2, 4, slab, 2 * hid), BF16),
        ((2, 4, slab, 2 * hid), BF16),
        ((2, 2, slab, feat), BF16),
        ((2, 2, 2, 2 * rows, feat), BF16),
        ((2, 2, 2, 2 * rows, feat), F32),
        ((2, 2, 2, slab, feat), BF16),
        ((2, 2, 2, slab, feat), BF16),
        ((2, 2, slab, feat), F32),
        ((2, 2, 3, rows, feat), BF16),
        ((2, 2, 3, rows, feat), BF16),
        ((2, 2, rows, feat), F32),
        ((2, rows, feat), BF16),
        ((2, rows, feat), BF16),
    ]
    return pl.pallas_call(
        kernel,
        out_shape=[
            pltpu.VMEM((rows, feat), BF16),
            pltpu.VMEM((rows, feat), BF16),
            pltpu.VMEM((feat, hid), F32),
            pltpu.VMEM((hid, feat), F32),
        ],
        in_specs=[hbm] * 4,
        out_specs=[vmem] * 4,
        scratch_shapes=[pltpu.VMEM(*s) for s in scratch] + [
            pltpu.SemaphoreType.DMA((N_REMOTE,)),
            pltpu.SemaphoreType.DMA((N_REMOTE,)),
            pltpu.SemaphoreType.DMA((N_LOCAL,)),
        ],
        compiler_params=pltpu.CompilerParams(
            collective_id=0, has_side_effects=True, vmem_limit_bytes=52 * 2**20
        ),
        name="exchange",
    )(tokens_in, w_in, w_out, grad_output)


def drain_kernel(*refs):
    n = len(refs) // 2
    copies = [pltpu.make_async_copy(refs[i], refs[n + i], refs[-1].at[i]) for i in range(n)]
    for copy in copies:
        copy.start()
    for copy in copies:
        copy.wait()


def drain(arrays):
    arrays = [pltpu.with_memory_space_constraint(a, pltpu.VMEM) for a in arrays]
    anywhere = [pl.BlockSpec(memory_space=pl.ANY)] * len(arrays)
    return pl.pallas_call(
        drain_kernel,
        out_shape=[pltpu.HBM(a.shape, a.dtype) for a in arrays],
        in_specs=anywhere,
        out_specs=anywhere,
        scratch_shapes=[pltpu.SemaphoreType.DMA((len(arrays),))],
        compiler_params=pltpu.CompilerParams(vmem_limit_bytes=2**20),
        name="drain",
    )(*arrays)


def per_device(*arrays):
    return tuple(drain(exchange(*arrays)))


def solution(mesh):
    placed = (
        P(("depth", "col"), "row"),
        P("row", ("depth", "col")),
        P(("depth", "col"), "row"),
        P(("depth", "col"), "row"),
    )
    return jax.shard_map(
        per_device,
        mesh=mesh,
        in_specs=placed,
        out_specs=(
            P(("depth", "col"), "row"),
            P(("depth", "col"), "row"),
            P("row", ("depth", "col")),
            P(("depth", "col"), "row"),
        ),
        check_vma=False,
    )
```

```python
import functools

import jax
import jax.numpy as jnp
from jax import lax
from jax.experimental import pallas as pl
from jax.experimental.pallas import tpu as pltpu
from jax.sharding import PartitionSpec as P

MESH = pl.DeviceIdType.MESH
BF16, F32 = jnp.bfloat16, jnp.float32
OFFSETS = (0, 1, 3, 2)
N_REMOTE = 160
N_LOCAL = 16


def contract_rows(left, right):
    return lax.dot_general(left, right, (((0,), (0,)), ((), ())), preferred_element_type=F32)


def nn(left, right):
    return jnp.dot(left, right, preferred_element_type=F32)


def nt(left, right):
    return lax.dot_general(left, right, (((1,), (1,)), ((), ())), preferred_element_type=F32)


def kernel(
    tokens, w_in, w_out, cotangent,
    out, gin, grad_in, grad_out,
    g_tok, g_cot, e_tok, e_cot, e_act, e_dpre, act_t, wi, wo, pre, dact, s_pre, r_pre, s_dact, r_dact, act, dpre,
    q2, r2, mid, s1, r1, acc, u2, v2, fin, s3, r3,
    send, recv, local,
):
    rows, feat = tokens.shape
    hid = w_in.shape[1]
    slab = 4 * rows
    depth, row, col = lax.axis_index("depth"), lax.axis_index("row"), lax.axis_index("col")
    low = lax.rem(col, 2)
    y = lax.rem(lax.div(col, 2), 4)
    z = lax.div(col, 8)

    def at(dy=0, dz=0, lo=None, r=None, d=None):
        c = lax.rem(z + dz, 4) * 8 + lax.rem(y + dy, 4) * 2 + (low if lo is None else lo)
        return (depth if d is None else d, row if r is None else r, c)

    x_partner = at(lo=1 - low)
    row_partner = at(r=1 - row)
    core_partner = at(d=1 - depth)
    along_y = {o: at(dy=o) for o in (1, 2, 3)}
    along_z = {o: at(dz=o) for o in (1, 2, 3)}
    ring1 = (along_z, along_y)
    ring2 = (along_y, along_z)
    own = (y, z)
    sub = (z, y)

    counter, counter_local, sent = [0], [0], []

    def remote(src, dst, device):
        i = counter[0]
        counter[0] += 1
        copy = pltpu.make_async_remote_copy(
            src_ref=src, dst_ref=dst, send_sem=send.at[i], recv_sem=recv.at[i],
            device_id=device, device_id_type=MESH,
        )
        copy.start()
        sent.append(copy)
        return copy

    def here(src, dst):
        i = counter_local[0]
        counter_local[0] += 1
        copy = pltpu.make_async_copy(src, dst, local.at[i])
        copy.start()
        return copy

    def piece(j):
        return pl.ds(pl.multiple_of(j * rows, rows), rows)

    def ring_at(h, o):
        return lax.rem(own[h] + o, 4)

    my_block = (low, y + low * (z - y), piece(z + low * (y - z)))
    own_copies = [here(tokens, g_tok.at[my_block]), here(cotangent, g_cot.at[my_block])]
    weight_copies = [
        here(w_in, wi.at[:, pl.ds(0, hid)]),
        here(w_out, wo.at[pl.ds(0, hid)]),
    ]

    barrier = pltpu.get_barrier_semaphore()
    friends = [x_partner, row_partner, core_partner] + list(along_y.values()) + list(along_z.values())
    for friend in friends:
        pl.semaphore_signal(barrier, inc=1, device_id=friend, device_id_type=MESH)
    pl.semaphore_wait(barrier, len(friends))

    def arrived(copies):
        for copy in copies:
            copy.wait_recv()

    def half_of(kind):
        return low if kind == 0 else 1 - low

    def place(kind, di, j):
        h = half_of(kind)
        i0, j0 = y + h * (z - y), z + h * (y - z)
        return h, lax.rem(i0 + di, 4), piece(lax.rem(j0 + j, 4))

    def to_ring1(kind, o):
        h = half_of(kind)
        return at(dy=o * h, dz=o * (1 - h))

    def to_ring2(kind, o):
        h = half_of(kind)
        return at(dy=o * (1 - h), dz=o * h)

    def gather_ring1(g, kind, src=None):
        block = g.at[place(kind, 0, 0)]
        return {o: remote(block if src is None else src, block, to_ring1(kind, o)) for o in (1, 3, 2)}

    def gather_ring2(g, kind, j, src=None):
        block = g.at[place(kind, 0, j)]
        return {o: remote(block if src is None else src, block, to_ring2(kind, o)) for o in (1, 3)}

    def gather_forward(g, kind, j, o):
        block = g.at[place(kind, 4 - o, j)]
        return remote(block, block, to_ring2(kind, o))

    own_src = {0: tokens, 1: cotangent}
    gathered = {0: g_tok, 1: g_cot}
    one, two, three = {}, {}, {}

    def start_own(k):
        one[k, 0] = gather_ring1(gathered[k], 0, own_src[k])
        two[k, 0, 0] = gather_ring2(gathered[k], 0, 0, own_src[k])

    def start_other(k):
        own_copies[k].wait()
        g0[k].wait_recv()
        one[k, 1] = gather_ring1(gathered[k], 1)
        two[k, 1, 0] = gather_ring2(gathered[k], 1, 0)

    def ring2_send(k, kind, j):
        one[k, kind][4 - j].wait_recv()
        two[k, kind, j] = gather_ring2(gathered[k], kind, j)

    def forward(k, kind, j, o):
        two[k, kind, j][o].wait_recv()
        three[k, kind, j, o] = gather_forward(gathered[k], kind, j, o)

    FORWARDS = ((0, 1), (1, 3), (3, 1), (2, 3))

    def gathered_near(k):
        for kind in range(2):
            for j in (0, 1, 3, 2):
                for o in (1, 3):
                    if (j, o) not in FORWARDS:
                        two[k, kind, j][o].wait_recv()

    def gathered_far(k):
        for kind in range(2):
            for j, o in FORWARDS:
                three[k, kind, j, o].wait_recv()

    g0 = [remote(tokens, g_tok.at[place(0, 0, 0)], x_partner)]
    start_own(0)
    g0.append(remote(cotangent, g_cot.at[place(0, 0, 0)], x_partner))
    weight_in = remote(w_in, wi.at[:, pl.ds(hid, hid)], core_partner)
    weight_out = remote(w_out, wo.at[pl.ds(hid, hid)], core_partner)
    start_other(0)
    one[1, 0] = gather_ring1(g_cot, 0, cotangent)

    tile = 256
    n_hid = 2 * hid // tile

    def rows_of(g, o):
        return jnp.concatenate([g[h, ring_at(h, o)] for h in range(2)], axis=0)

    def pre_step(s):
        chunk = rows_of(g_tok, OFFSETS[s])

        def body(t, _):
            cols = pl.ds(pl.multiple_of(t * tile, tile), tile)
            value = nn(chunk, wi[:, cols])
            pre[s, :, cols] = value
            s_pre[s, :, cols] = value.astype(BF16)
            return 0

        lax.fori_loop(0, n_hid, body, 0)
        return remote(s_pre.at[s], r_pre.at[s], row_partner)

    def dact_step(s):
        chunk = rows_of(g_cot, OFFSETS[s])

        def body(t, _):
            cols = pl.ds(pl.multiple_of(t * tile, tile), tile)
            value = nt(chunk, wo[cols, :])
            dact[s, :, cols] = value
            s_dact[s, :, cols] = value.astype(BF16)
            return 0

        lax.fori_loop(0, n_hid, body, 0)
        return remote(s_dact.at[s], r_dact.at[s], row_partner)

    def act_step(s, copy):
        copy.wait_recv()
        for h in range(2):
            i = ring_at(h, OFFSETS[s])

            def body(t, _):
                r_in = pl.ds(pl.multiple_of(h * slab + t * 16, 16), 16)
                r_out = pl.ds(pl.multiple_of(t * 16, 16), 16)
                hidden = pre[s, r_in, :] + r_pre[s, r_in, :].astype(F32)
                square = hidden * hidden
                inner = 0.7978845608 * (hidden + 0.044715 * square * hidden)
                tangent = jnp.tanh(inner)
                act[h, i, r_out, :] = (0.5 * hidden * (1.0 + tangent)).astype(BF16)
                pre[s, r_in, :] = 0.5 * (1.0 + tangent) + 0.5 * hidden * (
                    1.0 - tangent * tangent
                ) * 0.7978845608 * (1.0 + 3.0 * 0.044715 * square)
                return 0

            lax.fori_loop(0, slab // 16, body, 0)

    def dpre_step(s, copy):
        copy.wait_recv()
        for h in range(2):
            i = ring_at(h, OFFSETS[s])

            def body(t, _):
                r_in = pl.ds(pl.multiple_of(h * slab + t * 16, 16), 16)
                r_out = pl.ds(pl.multiple_of(t * 16, 16), 16)
                total = dact[s, r_in, :] + r_dact[s, r_in, :].astype(F32)
                dpre[h, i, r_out, :] = (total * pre[s, r_in, :]).astype(BF16)
                return 0

            lax.fori_loop(0, slab // 16, body, 0)

    wide = 512
    low_rows, high_rows = slice(0, 2 * rows), slice(2 * rows, 4 * rows)

    def span(f):
        return pl.ds(f[0] * (feat // f[1]), feat // f[1])

    def project(k, s, f):
        chunk = rows_of((act, dpre)[k], OFFSETS[s])
        o = OFFSETS[s]
        n = feat // f[1] // wide

        def body(t, _):
            cols = pl.ds(pl.multiple_of((f[0] * n + t) * wide, wide), wide)
            value = nn(chunk, wo[:, cols]) if k == 0 else nt(chunk, wi[cols, :])
            for h in range(2):
                part = value[h * slab:(h + 1) * slab]
                if o == 2:
                    q2[k, h, :, cols] = part.astype(BF16)
                elif o == 1:
                    s1[k, h, 0, high_rows, cols] = part[high_rows].astype(BF16)
                    mid[k, h, 0, :, cols] = part[low_rows]
                elif o == 3:
                    s1[k, h, 1, low_rows, cols] = part[low_rows].astype(BF16)
                    mid[k, h, 1, :, cols] = part[high_rows]
                else:
                    acc[k, h, :, cols] = part
            return 0

        lax.fori_loop(0, n, body, 0)

    far, near, merged, second, third = {}, {}, {}, {}, {}

    def scatter_far(k, f):
        project(k, 3, f)
        cols = span(f)
        far[k, f] = []
        for h in range(2):
            for side, part in enumerate((low_rows, high_rows)):
                far[k, f].append(remote(
                    q2.at[k, h, part, cols], r2.at[k, h, side, :, cols], ring2[h][(1, 3)[side]]
                ))

    def scatter_near(k, f, side):
        project(k, 1 + side, f)
        part = (high_rows, low_rows)[side]
        cols = span(f)
        near.setdefault((k, f), []).extend(
            remote(s1.at[k, h, side, part, cols], r1.at[k, h, side, part, cols], ring2[h][(1, 3)[side]])
            for h in range(2)
        )

    def scatter_merge(k, f):
        cols = span(f)
        merged[k, f] = []
        for h in range(2):
            for side in range(2):
                far[k, f][2 * h + side].wait_recv()
                base = side * 2 * rows

                def body(t, _):
                    r_in = pl.ds(pl.multiple_of(t * 16, 16), 16)
                    r_out = pl.ds(pl.multiple_of(base + t * 16, 16), 16)
                    total = mid[k, h, side, r_in, cols] + r2[k, h, side, r_in, cols].astype(F32)
                    s1[k, h, side, r_out, cols] = total.astype(BF16)
                    return 0

                lax.fori_loop(0, 2 * rows // 16, body, 0)
                part = (low_rows, high_rows)[side]
                merged[k, f].append(remote(
                    s1.at[k, h, side, part, cols], r1.at[k, h, side, part, cols],
                    ring2[h][(1, 3)[side]],
                ))

    def scatter_two(k, f):
        cols = span(f)
        arrived(near[k, f])
        arrived(merged[k, f])
        second[k, f] = []
        for h in range(2):
            for slot, o in enumerate((2, 1, 3)):
                r_in = piece(lax.rem(sub[h] + o, 4))
                total = acc[k, h, r_in, cols] + r1[k, h, 0, r_in, cols].astype(F32)
                u2[k, h, slot, :, cols] = (total + r1[k, h, 1, r_in, cols].astype(F32)).astype(BF16)
                second[k, f].append(remote(
                    u2.at[k, h, slot, :, cols], v2.at[k, h, slot, :, cols], ring1[h][o]
                ))

    def scatter_three(k, f):
        cols = span(f)
        arrived(second[k, f])
        for h in range(2):
            r_in = piece(sub[h])
            total = acc[k, h, r_in, cols] + r1[k, h, 0, r_in, cols].astype(F32)
            total += r1[k, h, 1, r_in, cols].astype(F32)
            for slot in range(3):
                total += v2[k, h, slot, :, cols].astype(F32)
            fin[k, h, :, cols] = total
        s3[k, :, cols] = fin[k, 1 - low, :, cols].astype(BF16)
        third[k, f] = remote(s3.at[k, :, cols], r3.at[k, :, cols], x_partner)

    def finish(k, f):
        cols = span(f)
        third[k, f].wait_recv()
        (out, gin)[k][:, cols] = (fin[k, low, :, cols] + r3[k, :, cols].astype(F32)).astype(BF16)

    mine, other = pl.ds(0, hid), pl.ds(hid, hid)
    tokens_all = 8 * slab

    def flat(value):
        return value.reshape(tokens_all, value.shape[-1])

    def turn_act():
        act_t[0] = jnp.transpose(flat(act[:, :, :, mine]))
        act_t[1] = jnp.transpose(flat(e_act[...]))

    def grad_out_part(start, stop):
        def body(t, _):
            cols = pl.ds(pl.multiple_of(t * tile, tile), tile)
            value = nn(act_t[0], flat(g_cot[:, :, :, cols]))
            grad_out[:, cols] = value + nn(act_t[1], flat(e_cot[:, :, :, cols]))
            return 0

        lax.fori_loop(start, stop, body, 0)

    def grad_in_part(start, stop):
        def body(t, _):
            cols = pl.ds(pl.multiple_of(t * tile, tile), tile)
            value = contract_rows(flat(g_tok[:, :, :, cols]), flat(dpre[:, :, :, mine]))
            value += contract_rows(flat(e_tok[:, :, :, cols]), flat(e_dpre[...]))
            grad_in[cols, :] = value
            return 0

        lax.fori_loop(start, stop, body, 0)

    forward(0, 0, 0, 1)
    ring2_send(0, 0, 1)
    ring2_send(0, 0, 3)
    ring2_send(0, 0, 2)
    ring2_send(0, 1, 1)
    ring2_send(0, 1, 3)
    ring2_send(0, 1, 2)
    forward(0, 1, 0, 1)
    weight_copies[0].wait()
    weight_in.wait_recv()
    p = {0: pre_step(0)}
    forward(0, 0, 1, 3)
    forward(0, 1, 1, 3)
    forward(0, 0, 3, 1)
    forward(0, 0, 2, 3)
    own_copies[1].wait()
    g0[1].wait_recv()
    one[1, 1] = gather_ring1(g_cot, 1)
    forward(0, 1, 3, 1)
    forward(0, 1, 2, 3)
    two[1, 0, 0] = gather_ring2(g_cot, 0, 0)
    two[1, 1, 0] = gather_ring2(g_cot, 1, 0)
    ring2_send(1, 0, 1)
    ring2_send(1, 0, 3)
    ring2_send(1, 0, 2)
    gathered_near(0)
    p[1] = pre_step(1)
    gathered_far(0)
    p[3] = pre_step(3)
    p[2] = pre_step(2)
    every_tok = remote(g_tok, e_tok, core_partner)
    forward(1, 0, 0, 1)
    ring2_send(1, 1, 1)
    ring2_send(1, 1, 3)
    ring2_send(1, 1, 2)
    forward(1, 1, 0, 1)
    weight_copies[1].wait()
    weight_out.wait_recv()
    q = {0: dact_step(0)}
    act_step(0, p[0])
    forward(1, 0, 1, 3)
    forward(1, 1, 1, 3)
    forward(1, 0, 3, 1)
    forward(1, 1, 3, 1)
    forward(1, 0, 2, 3)
    act_step(1, p[1])
    act_step(3, p[3])
    forward(1, 1, 2, 3)
    whole, first, last = (0, 1), (0, 2), (1, 2)
    scatter_far(0, whole)
    scatter_near(0, whole, 0)
    gathered_near(1)
    gathered_far(1)
    q[3] = dact_step(3)
    act_step(2, p[2])
    scatter_near(0, whole, 1)
    every_act = remote(act.at[:, :, :, other], e_act, core_partner)
    q[1] = dact_step(1)
    scatter_merge(0, whole)
    q[2] = dact_step(2)
    every_cot = remote(g_cot, e_cot, core_partner)
    dpre_step(3, q[3])
    scatter_far(1, first)
    scatter_far(1, last)
    project(0, 0, whole)
    dpre_step(1, q[1])
    scatter_near(1, first, 0)
    scatter_two(0, whole)
    scatter_near(1, last, 0)
    dpre_step(2, q[2])
    scatter_near(1, first, 1)
    scatter_merge(1, first)
    scatter_near(1, last, 1)
    scatter_merge(1, last)
    dpre_step(0, q[0])
    every_dpre = remote(dpre.at[:, :, :, other], e_dpre, core_partner)
    project(1, 0, whole)
    every_act.wait_recv()
    turn_act()
    every_cot.wait_recv()
    grad_out_part(0, 4)
    scatter_three(0, whole)
    grad_out_part(4, 8)
    scatter_two(1, first)
    grad_out_part(8, 12)
    finish(0, whole)
    scatter_two(1, last)
    every_tok.wait_recv()
    every_dpre.wait_recv()
    grad_in_part(0, 4)
    scatter_three(1, first)
    grad_in_part(4, 8)
    scatter_three(1, last)
    grad_in_part(8, 12)
    finish(1, first)
    finish(1, last)
    for copy in sent:
        copy.wait_send()


def exchange(tokens_in, w_in, w_out, grad_output):
    rows, feat = tokens_in.shape
    hid = w_in.shape[1]
    slab = 4 * rows
    vmem, hbm = pl.BlockSpec(memory_space=pltpu.VMEM), pl.BlockSpec(memory_space=pl.ANY)
    scratch = [
        ((2, 4, slab, feat), BF16),
        ((2, 4, slab, feat), BF16),
        ((2, 4, slab, feat), BF16),
        ((2, 4, slab, feat), BF16),
        ((2, 4, slab, hid), BF16),
        ((2, 4, slab, hid), BF16),
        ((2, hid, 8 * slab), BF16),
        ((feat, 2 * hid), BF16),
        ((2 * hid, feat), BF16),
        ((4, 2 * slab, 2 * hid), F32),
        ((4, 2 * slab, 2 * hid), F32),
        ((4, 2 * slab, 2 * hid), BF16),
        ((4, 2 * slab, 2 * hid), BF16),
        ((4, 2 * slab, 2 * hid), BF16),
        ((4, 2 * slab, 2 * hid), BF16),
        ((2, 4, slab, 2 * hid), BF16),
        ((2, 4, slab, 2 * hid), BF16),
        ((2, 2, slab, feat), BF16),
        ((2, 2, 2, 2 * rows, feat), BF16),
        ((2, 2, 2, 2 * rows, feat), F32),
        ((2, 2, 2, slab, feat), BF16),
        ((2, 2, 2, slab, feat), BF16),
        ((2, 2, slab, feat), F32),
        ((2, 2, 3, rows, feat), BF16),
        ((2, 2, 3, rows, feat), BF16),
        ((2, 2, rows, feat), F32),
        ((2, rows, feat), BF16),
        ((2, rows, feat), BF16),
    ]
    return pl.pallas_call(
        kernel,
        out_shape=[
            pltpu.VMEM((rows, feat), BF16),
            pltpu.VMEM((rows, feat), BF16),
            pltpu.VMEM((feat, hid), F32),
            pltpu.VMEM((hid, feat), F32),
        ],
        in_specs=[hbm] * 4,
        out_specs=[vmem] * 4,
        scratch_shapes=[pltpu.VMEM(*s) for s in scratch] + [
            pltpu.SemaphoreType.DMA((N_REMOTE,)),
            pltpu.SemaphoreType.DMA((N_REMOTE,)),
            pltpu.SemaphoreType.DMA((N_LOCAL,)),
        ],
        compiler_params=pltpu.CompilerParams(
            collective_id=0, has_side_effects=True, vmem_limit_bytes=52 * 2**20
        ),
        name="exchange",
    )(tokens_in, w_in, w_out, grad_output)


def drain_kernel(*refs):
    n = len(refs) // 2
    copies = [pltpu.make_async_copy(refs[i], refs[n + i], refs[-1].at[i]) for i in range(n)]
    for copy in copies:
        copy.start()
    for copy in copies:
        copy.wait()


def drain(arrays):
    arrays = [pltpu.with_memory_space_constraint(a, pltpu.VMEM) for a in arrays]
    anywhere = [pl.BlockSpec(memory_space=pl.ANY)] * len(arrays)
    return pl.pallas_call(
        drain_kernel,
        out_shape=[pltpu.HBM(a.shape, a.dtype) for a in arrays],
        in_specs=anywhere,
        out_specs=anywhere,
        scratch_shapes=[pltpu.SemaphoreType.DMA((len(arrays),))],
        compiler_params=pltpu.CompilerParams(vmem_limit_bytes=2**20),
        name="drain",
    )(*arrays)


def per_device(*arrays):
    return tuple(drain(exchange(*arrays)))


def solution(mesh):
    placed = (
        P(("depth", "col"), "row"),
        P("row", ("depth", "col")),
        P(("depth", "col"), "row"),
        P(("depth", "col"), "row"),
    )
    return jax.shard_map(
        per_device,
        mesh=mesh,
        in_specs=placed,
        out_specs=(
            P(("depth", "col"), "row"),
            P(("depth", "col"), "row"),
            P("row", ("depth", "col")),
            P(("depth", "col"), "row"),
        ),
        check_vma=False,
    )
```

```python
import functools

import jax
import jax.numpy as jnp
from jax import lax
from jax.experimental import pallas as pl
from jax.experimental.pallas import tpu as pltpu
from jax.sharding import PartitionSpec as P

MESH = pl.DeviceIdType.MESH
BF16, F32 = jnp.bfloat16, jnp.float32
OFFSETS = (0, 1, 3, 2)
N_REMOTE = 160
N_LOCAL = 16


def contract_rows(left, right):
    return lax.dot_general(left, right, (((0,), (0,)), ((), ())), preferred_element_type=F32)


def nn(left, right):
    return jnp.dot(left, right, preferred_element_type=F32)


def nt(left, right):
    return lax.dot_general(left, right, (((1,), (1,)), ((), ())), preferred_element_type=F32)


def kernel(
    tokens, w_in, w_out, cotangent,
    out, gin, grad_in, grad_out,
    g_tok, g_cot, e_tok, e_cot, e_act, e_dpre, act_t, wi, wo, pre, dact, s_pre, r_pre, s_dact, r_dact, act, dpre,
    q2, r2, mid, s1, r1, acc, u2, v2, fin, s3, r3,
    send, recv, local,
):
    rows, feat = tokens.shape
    hid = w_in.shape[1]
    slab = 4 * rows
    depth, row, col = lax.axis_index("depth"), lax.axis_index("row"), lax.axis_index("col")
    low = lax.rem(col, 2)
    y = lax.rem(lax.div(col, 2), 4)
    z = lax.div(col, 8)

    def at(dy=0, dz=0, lo=None, r=None, d=None):
        c = lax.rem(z + dz, 4) * 8 + lax.rem(y + dy, 4) * 2 + (low if lo is None else lo)
        return (depth if d is None else d, row if r is None else r, c)

    x_partner = at(lo=1 - low)
    row_partner = at(r=1 - row)
    core_partner = at(d=1 - depth)
    along_y = {o: at(dy=o) for o in (1, 2, 3)}
    along_z = {o: at(dz=o) for o in (1, 2, 3)}
    ring1 = (along_z, along_y)
    ring2 = (along_y, along_z)
    own = (y, z)
    sub = (z, y)

    counter, counter_local, sent, seen = [0], [0], [], set()

    def remote(src, dst, device):
        i = counter[0]
        counter[0] += 1
        copy = pltpu.make_async_remote_copy(
            src_ref=src, dst_ref=dst, send_sem=send.at[i], recv_sem=recv.at[i],
            device_id=device, device_id_type=MESH,
        )
        copy.start()
        sent.append(copy)
        return copy

    def here(src, dst):
        i = counter_local[0]
        counter_local[0] += 1
        copy = pltpu.make_async_copy(src, dst, local.at[i])
        copy.start()
        return copy

    def piece(j):
        return pl.ds(pl.multiple_of(j * rows, rows), rows)

    def ring_at(h, o):
        return lax.rem(own[h] + o, 4)

    my_block = (low, y + low * (z - y), piece(z + low * (y - z)))
    own_copies = [here(tokens, g_tok.at[my_block]), here(cotangent, g_cot.at[my_block])]
    weight_copies = [
        here(w_in, wi.at[:, pl.ds(0, hid)]),
        here(w_out, wo.at[pl.ds(0, hid)]),
    ]

    barrier = pltpu.get_barrier_semaphore()
    friends = [x_partner, row_partner, core_partner] + list(along_y.values()) + list(along_z.values())
    for friend in friends:
        pl.semaphore_signal(barrier, inc=1, device_id=friend, device_id_type=MESH)
    pl.semaphore_wait(barrier, len(friends))

    def arrived(copies):
        for copy in copies:
            if id(copy) not in seen:
                seen.add(id(copy))
                copy.wait_recv()

    def landed(copy):
        if id(copy) not in seen:
            seen.add(id(copy))
            copy.wait()

    def half_of(kind):
        return low if kind == 0 else 1 - low

    def place(kind, di, j):
        h = half_of(kind)
        i0, j0 = y + h * (z - y), z + h * (y - z)
        return h, lax.rem(i0 + di, 4), piece(lax.rem(j0 + j, 4))

    def to_ring1(kind, o):
        h = half_of(kind)
        return at(dy=o * h, dz=o * (1 - h))

    def to_ring2(kind, o):
        h = half_of(kind)
        return at(dy=o * (1 - h), dz=o * h)

    own_src = {0: tokens, 1: cotangent}
    gathered = {0: g_tok, 1: g_cot}
    g0, one, two, three = {}, {}, {}, {}
    FORWARDS = ((0, 1), (1, 3), (3, 1), (2, 3))

    def send_x(k):
        g0[k] = remote(own_src[k], gathered[k].at[place(0, 0, 0)], x_partner)

    def source(k, kind, block):
        if kind == 0:
            return own_src[k]
        arrived([g0[k]])
        return block

    def ring1_send(k, kind):
        block = gathered[k].at[place(kind, 0, 0)]
        src = source(k, kind, block)
        one[k, kind] = {o: remote(src, block, to_ring1(kind, o)) for o in (1, 3)}

    def ring1_forward(k, kind):
        for o in (1, 3):
            arrived([one[k, kind][o]])
            h, i, r = place(kind, 0, 4 - o)
            block = gathered[k].at[h, i, r, pl.ds((o // 2) * (feat // 2), feat // 2)]
            one[k, kind, o] = remote(block, block, to_ring1(kind, o))

    def ring2_send(k, kind, j):
        block = gathered[k].at[place(kind, 0, j)]
        src = block
        if j == 0:
            src = source(k, kind, block)
        elif j == 2:
            arrived([one[k, kind, 1], one[k, kind, 3]])
        else:
            arrived([one[k, kind][4 - j]])
        two[k, kind, j] = {o: remote(src, block, to_ring2(kind, o)) for o in (1, 3)}

    def forward(k, kind, j, o):
        arrived([two[k, kind, j][o]])
        block = gathered[k].at[place(kind, 4 - o, j)]
        three[k, kind, j, o] = remote(block, block, to_ring2(kind, o))

    def gathered_side(k, o):
        for kind in range(2):
            for j in range(4):
                if (j, o) not in FORWARDS:
                    arrived([two[k, kind, j][o]])

    def gathered_far(k):
        for kind in range(2):
            for j, o in FORWARDS:
                arrived([three[k, kind, j, o]])

    for copy in own_copies:
        landed(copy)

    core, p, q = {}, {}, {}
    tile = feat // 3

    def send_weights():
        core["w_in"] = remote(w_in, wi.at[:, pl.ds(hid, hid)], core_partner)
        core["w_out"] = remote(w_out, wo.at[pl.ds(hid, hid)], core_partner)

    def rows_of(g, o):
        return jnp.concatenate([g[h, ring_at(h, o)] for h in range(2)], axis=0)

    def pre_step(s):
        landed(weight_copies[0])
        arrived([core["w_in"]])
        value = nn(rows_of(g_tok, OFFSETS[s]), wi[...])
        pre[s] = value
        s_pre[s] = value.astype(BF16)
        p[s] = remote(s_pre.at[s], r_pre.at[s], row_partner)

    def dact_step(s):
        landed(weight_copies[1])
        arrived([core["w_out"]])
        value = nt(rows_of(g_cot, OFFSETS[s]), wo[...])
        dact[s] = value
        s_dact[s] = value.astype(BF16)
        q[s] = remote(s_dact.at[s], r_dact.at[s], row_partner)

    def act_step(s):
        arrived([p[s]])
        for h in range(2):
            i = ring_at(h, OFFSETS[s])

            def body(t, _):
                r_in = pl.ds(pl.multiple_of(h * slab + t * 16, 16), 16)
                r_out = pl.ds(pl.multiple_of(t * 16, 16), 16)
                hidden = pre[s, r_in, :] + r_pre[s, r_in, :].astype(F32)
                square = hidden * hidden
                inner = 0.7978845608 * (hidden + 0.044715 * square * hidden)
                tangent = jnp.tanh(inner)
                act[h, i, r_out, :] = (0.5 * hidden * (1.0 + tangent)).astype(BF16)
                pre[s, r_in, :] = 0.5 * (1.0 + tangent) + 0.5 * hidden * (
                    1.0 - tangent * tangent
                ) * 0.7978845608 * (1.0 + 3.0 * 0.044715 * square)
                return 0

            lax.fori_loop(0, slab // 16, body, 0)

    def dpre_step(s):
        arrived([q[s]])
        for h in range(2):
            i = ring_at(h, OFFSETS[s])

            def body(t, _):
                r_in = pl.ds(pl.multiple_of(h * slab + t * 16, 16), 16)
                r_out = pl.ds(pl.multiple_of(t * 16, 16), 16)
                total = dact[s, r_in, :] + r_dact[s, r_in, :].astype(F32)
                dpre[h, i, r_out, :] = (total * pre[s, r_in, :]).astype(BF16)
                return 0

            lax.fori_loop(0, slab // 16, body, 0)

    low_rows, high_rows = slice(0, 2 * rows), slice(2 * rows, 4 * rows)

    def span(f):
        return pl.ds(f[0] * (feat // 6), f[1] * (feat // 6))

    def project(k, s, f):
        chunk = rows_of((act, dpre)[k], OFFSETS[s])
        o = OFFSETS[s]
        cols = span(f)
        landed(weight_copies[k - 1])
        arrived([core[("w_out", "w_in")[k]]])
        value = nn(chunk, wo[:, cols]) if k == 0 else nt(chunk, wi[cols, :])
        for h in range(2):
            part = value[h * slab:(h + 1) * slab]
            if o == 2:
                q2[k, h, :, cols] = part.astype(BF16)
            elif o == 1:
                s1[k, h, 0, high_rows, cols] = part[high_rows].astype(BF16)
                mid[k, h, 0, :, cols] = part[low_rows]
            elif o == 3:
                s1[k, h, 1, low_rows, cols] = part[low_rows].astype(BF16)
                mid[k, h, 1, :, cols] = part[high_rows]
            else:
                acc[k, h, :, cols] = part

    far, near, merged, second, third = {}, {}, {}, {}, {}

    def scatter_far(k, f):
        project(k, 3, f)
        cols = span(f)
        far[k, f] = []
        for h in range(2):
            for side, part in enumerate((low_rows, high_rows)):
                far[k, f].append(remote(
                    q2.at[k, h, part, cols], r2.at[k, h, side, :, cols], ring2[h][(1, 3)[side]]
                ))

    def scatter_near(k, f, side):
        project(k, 1 + side, f)
        part = (high_rows, low_rows)[side]
        cols = span(f)
        near.setdefault((k, f), []).extend(
            remote(s1.at[k, h, side, part, cols], r1.at[k, h, side, part, cols], ring2[h][(1, 3)[side]])
            for h in range(2)
        )

    def scatter_merge(k, f):
        cols = span(f)
        merged[k, f] = []
        for h in range(2):
            for side in range(2):
                arrived([far[k, f][2 * h + side]])
                base = side * 2 * rows

                def body(t, _):
                    r_in = pl.ds(pl.multiple_of(t * 16, 16), 16)
                    r_out = pl.ds(pl.multiple_of(base + t * 16, 16), 16)
                    total = mid[k, h, side, r_in, cols] + r2[k, h, side, r_in, cols].astype(F32)
                    s1[k, h, side, r_out, cols] = total.astype(BF16)
                    return 0

                lax.fori_loop(0, 2 * rows // 16, body, 0)
                part = (low_rows, high_rows)[side]
                merged[k, f].append(remote(
                    s1.at[k, h, side, part, cols], r1.at[k, h, side, part, cols],
                    ring2[h][(1, 3)[side]],
                ))

    def scatter_two(k, f):
        cols = span(f)
        arrived(near[k, f])
        arrived(merged[k, f])
        second[k, f] = []
        for h in range(2):
            for slot, o in enumerate((2, 1, 3)):
                r_in = piece(lax.rem(sub[h] + o, 4))
                total = acc[k, h, r_in, cols] + r1[k, h, 0, r_in, cols].astype(F32)
                u2[k, h, slot, :, cols] = (total + r1[k, h, 1, r_in, cols].astype(F32)).astype(BF16)
                second[k, f].append(remote(
                    u2.at[k, h, slot, :, cols], v2.at[k, h, slot, :, cols], ring1[h][o]
                ))

    def scatter_three(k, f):
        cols = span(f)
        arrived(second[k, f])
        for h in range(2):
            r_in = piece(sub[h])
            total = acc[k, h, r_in, cols] + r1[k, h, 0, r_in, cols].astype(F32)
            total += r1[k, h, 1, r_in, cols].astype(F32)
            for slot in range(3):
                total += v2[k, h, slot, :, cols].astype(F32)
            fin[k, h, :, cols] = total
        s3[k, :, cols] = fin[k, 1 - low, :, cols].astype(BF16)
        third[k, f] = remote(s3.at[k, :, cols], r3.at[k, :, cols], x_partner)

    def finish(k, f):
        cols = span(f)
        arrived([third[k, f]])
        (out, gin)[k][:, cols] = (fin[k, low, :, cols] + r3[k, :, cols].astype(F32)).astype(BF16)

    mine, other = pl.ds(0, hid), pl.ds(hid, hid)
    tokens_all = 8 * slab

    def flat(value):
        return value.reshape(tokens_all, value.shape[-1])

    def send_core(name):
        src, dst = {
            "tok": (g_tok, e_tok),
            "cot": (g_cot, e_cot),
            "act": (act.at[:, :, :, other], e_act),
            "dpre": (dpre.at[:, :, :, other], e_dpre),
        }[name]
        core[name] = remote(src, dst, core_partner)

    def turn_act():
        arrived([core["act"]])
        act_t[0] = jnp.transpose(flat(act[:, :, :, mine]))
        act_t[1] = jnp.transpose(flat(e_act[...]))

    def grad_out_part(start, stop):
        arrived([core["cot"]])

        def body(t, _):
            cols = pl.ds(pl.multiple_of(t * tile, tile), tile)
            value = nn(act_t[0], flat(g_cot[:, :, :, cols]))
            grad_out[:, cols] = value + nn(act_t[1], flat(e_cot[:, :, :, cols]))
            return 0

        lax.fori_loop(start, stop, body, 0)

    def grad_in_part(start, stop):
        arrived([core["tok"], core["dpre"]])

        def body(t, _):
            cols = pl.ds(pl.multiple_of(t * tile, tile), tile)
            value = contract_rows(flat(g_tok[:, :, :, cols]), flat(dpre[:, :, :, mine]))
            value += contract_rows(flat(e_tok[:, :, :, cols]), flat(e_dpre[...]))
            grad_in[cols, :] = value
            return 0

        lax.fori_loop(start, stop, body, 0)

    whole, first, last = (0, 6), (0, 4), (4, 2)
    send_x(0)
    ring1_send(0, 0)
    ring2_send(1, 0, 0)
    ring1_send(1, 0)
    send_weights()
    ring2_send(0, 0, 0)
    ring1_send(0, 1)
    ring1_forward(0, 0)
    ring2_send(0, 0, 1)
    ring2_send(0, 1, 0)
    ring1_forward(1, 0)
    ring1_forward(0, 1)
    ring2_send(0, 1, 3)
    ring2_send(0, 0, 2)
    ring2_send(0, 0, 3)
    send_x(1)
    ring2_send(0, 1, 1)
    ring2_send(0, 1, 2)
    ring1_send(1, 1)
    pre_step(0)
    forward(0, 0, 0, 1)
    forward(0, 0, 2, 3)
    forward(0, 1, 1, 3)
    forward(0, 1, 3, 1)
    forward(0, 0, 1, 3)
    forward(0, 1, 0, 1)
    forward(0, 0, 3, 1)
    forward(0, 1, 2, 3)
    ring2_send(1, 1, 0)
    gathered_side(0, 3)
    gathered_side(0, 1)
    pre_step(1)
    ring1_forward(1, 1)
    ring2_send(1, 1, 1)
    ring2_send(1, 0, 3)
    forward(1, 0, 0, 1)
    gathered_far(0)
    pre_step(3)
    ring2_send(1, 1, 3)
    send_core("tok")
    ring2_send(1, 0, 2)
    pre_step(2)
    ring2_send(1, 1, 2)
    forward(1, 0, 3, 1)
    forward(1, 1, 0, 1)
    ring2_send(1, 0, 1)
    act_step(0)
    act_step(1)
    forward(1, 0, 2, 3)
    forward(1, 1, 3, 1)
    forward(1, 1, 1, 3)
    project(0, 0, whole)
    act_step(3)
    forward(1, 1, 2, 3)
    forward(1, 0, 1, 3)
    scatter_far(0, whole)
    gathered_side(1, 3)
    dact_step(1)
    scatter_near(0, whole, 0)
    act_step(2)
    scatter_near(0, whole, 1)
    gathered_far(1)
    dact_step(3)
    gathered_side(1, 1)
    dact_step(2)
    send_core("act")
    scatter_merge(0, whole)
    send_core("cot")
    dact_step(0)
    dpre_step(3)
    scatter_far(1, last)
    scatter_far(1, first)
    turn_act()
    dpre_step(1)
    scatter_two(0, whole)
    scatter_near(1, first, 0)
    dpre_step(2)
    scatter_near(1, first, 1)
    scatter_merge(1, first)
    scatter_near(1, last, 0)
    dpre_step(0)
    scatter_near(1, last, 1)
    send_core("dpre")
    scatter_merge(1, last)
    scatter_three(0, whole)
    project(1, 0, whole)
    grad_in_part(1, 2)
    scatter_two(1, first)
    grad_out_part(1, 2)
    scatter_two(1, last)
    grad_out_part(2, 3)
    grad_out_part(0, 1)
    finish(0, whole)
    scatter_three(1, first)
    scatter_three(1, last)
    grad_in_part(2, 3)
    grad_in_part(0, 1)
    finish(1, first)
    finish(1, last)
    for copy in sent:
        copy.wait_send()


def exchange(tokens_in, w_in, w_out, grad_output):
    rows, feat = tokens_in.shape
    hid = w_in.shape[1]
    slab = 4 * rows
    vmem, hbm = pl.BlockSpec(memory_space=pltpu.VMEM), pl.BlockSpec(memory_space=pl.ANY)
    scratch = [
        ((2, 4, slab, feat), BF16),
        ((2, 4, slab, feat), BF16),
        ((2, 4, slab, feat), BF16),
        ((2, 4, slab, feat), BF16),
        ((2, 4, slab, hid), BF16),
        ((2, 4, slab, hid), BF16),
        ((2, hid, 8 * slab), BF16),
        ((feat, 2 * hid), BF16),
        ((2 * hid, feat), BF16),
        ((4, 2 * slab, 2 * hid), F32),
        ((4, 2 * slab, 2 * hid), F32),
        ((4, 2 * slab, 2 * hid), BF16),
        ((4, 2 * slab, 2 * hid), BF16),
        ((4, 2 * slab, 2 * hid), BF16),
        ((4, 2 * slab, 2 * hid), BF16),
        ((2, 4, slab, 2 * hid), BF16),
        ((2, 4, slab, 2 * hid), BF16),
        ((2, 2, slab, feat), BF16),
        ((2, 2, 2, 2 * rows, feat), BF16),
        ((2, 2, 2, 2 * rows, feat), F32),
        ((2, 2, 2, slab, feat), BF16),
        ((2, 2, 2, slab, feat), BF16),
        ((2, 2, slab, feat), F32),
        ((2, 2, 3, rows, feat), BF16),
        ((2, 2, 3, rows, feat), BF16),
        ((2, 2, rows, feat), F32),
        ((2, rows, feat), BF16),
        ((2, rows, feat), BF16),
    ]
    return pl.pallas_call(
        kernel,
        out_shape=[
            pltpu.VMEM((rows, feat), BF16),
            pltpu.VMEM((rows, feat), BF16),
            pltpu.VMEM((feat, hid), F32),
            pltpu.VMEM((hid, feat), F32),
        ],
        in_specs=[hbm] * 4,
        out_specs=[vmem] * 4,
        scratch_shapes=[pltpu.VMEM(*s) for s in scratch] + [
            pltpu.SemaphoreType.DMA((N_REMOTE,)),
            pltpu.SemaphoreType.DMA((N_REMOTE,)),
            pltpu.SemaphoreType.DMA((N_LOCAL,)),
        ],
        compiler_params=pltpu.CompilerParams(
            collective_id=0, has_side_effects=True, vmem_limit_bytes=52 * 2**20
        ),
        name="exchange",
    )(tokens_in, w_in, w_out, grad_output)


def drain_kernel(*refs):
    n = len(refs) // 2
    copies = [pltpu.make_async_copy(refs[i], refs[n + i], refs[-1].at[i]) for i in range(n)]
    for copy in copies:
        copy.start()
    for copy in copies:
        copy.wait()


def drain(arrays):
    arrays = [pltpu.with_memory_space_constraint(a, pltpu.VMEM) for a in arrays]
    anywhere = [pl.BlockSpec(memory_space=pl.ANY)] * len(arrays)
    return pl.pallas_call(
        drain_kernel,
        out_shape=[pltpu.HBM(a.shape, a.dtype) for a in arrays],
        in_specs=anywhere,
        out_specs=anywhere,
        scratch_shapes=[pltpu.SemaphoreType.DMA((len(arrays),))],
        compiler_params=pltpu.CompilerParams(vmem_limit_bytes=2**20),
        name="drain",
    )(*arrays)


def per_device(*arrays):
    return tuple(drain(exchange(*arrays)))


def solution(mesh):
    placed = (
        P(("depth", "col"), "row"),
        P("row", ("depth", "col")),
        P(("depth", "col"), "row"),
        P(("depth", "col"), "row"),
    )
    return jax.shard_map(
        per_device,
        mesh=mesh,
        in_specs=placed,
        out_specs=(
            P(("depth", "col"), "row"),
            P(("depth", "col"), "row"),
            P("row", ("depth", "col")),
            P(("depth", "col"), "row"),
        ),
        check_vma=False,
    )
```

```python
import functools

import jax
import jax.numpy as jnp
from jax import lax
from jax.experimental import pallas as pl
from jax.experimental.pallas import tpu as pltpu
from jax.sharding import PartitionSpec as P

MESH = pl.DeviceIdType.MESH
BF16, F32 = jnp.bfloat16, jnp.float32
OFFSETS = (0, 1, 3, 2)
N_REMOTE = 176
N_LOCAL = 16


def contract_rows(left, right):
    return lax.dot_general(left, right, (((0,), (0,)), ((), ())), preferred_element_type=F32)


def nn(left, right):
    return jnp.dot(left, right, preferred_element_type=F32)


def nt(left, right):
    return lax.dot_general(left, right, (((1,), (1,)), ((), ())), preferred_element_type=F32)


def kernel(
    tokens, w_in, w_out, cotangent,
    out, gin, grad_in, grad_out,
    g_tok, g_cot, e_tok, e_cot, e_act, e_dpre, act_t, wi, wo, pre, dact, s_pre, r_pre, s_dact, r_dact, act, dpre,
    q2, r2, mid, s1, r1, acc, u2, v2, fin, s3, r3,
    send, recv, local,
):
    rows, feat = tokens.shape
    hid = w_in.shape[1]
    slab = 4 * rows
    depth, row, col = lax.axis_index("depth"), lax.axis_index("row"), lax.axis_index("col")
    low = lax.rem(col, 2)
    y = lax.rem(lax.div(col, 2), 4)
    z = lax.div(col, 8)

    def at(dy=0, dz=0, lo=None, r=None, d=None):
        c = lax.rem(z + dz, 4) * 8 + lax.rem(y + dy, 4) * 2 + (low if lo is None else lo)
        return (depth if d is None else d, row if r is None else r, c)

    x_partner = at(lo=1 - low)
    row_partner = at(r=1 - row)
    core_partner = at(d=1 - depth)
    along_y = {o: at(dy=o) for o in (1, 2, 3)}
    along_z = {o: at(dz=o) for o in (1, 2, 3)}
    ring1 = (along_z, along_y)
    ring2 = (along_y, along_z)
    own = (y, z)
    sub = (z, y)

    counter, counter_local, sent, seen = [0], [0], [], set()

    def remote(src, dst, device):
        i = counter[0]
        counter[0] += 1
        copy = pltpu.make_async_remote_copy(
            src_ref=src, dst_ref=dst, send_sem=send.at[i], recv_sem=recv.at[i],
            device_id=device, device_id_type=MESH,
        )
        copy.start()
        sent.append(copy)
        return copy

    def here(src, dst):
        i = counter_local[0]
        counter_local[0] += 1
        copy = pltpu.make_async_copy(src, dst, local.at[i])
        copy.start()
        return copy

    def piece(j):
        return pl.ds(pl.multiple_of(j * rows, rows), rows)

    def ring_at(h, o):
        return lax.rem(own[h] + o, 4)

    my_block = (low, y + low * (z - y), piece(z + low * (y - z)))
    own_copies = [here(tokens, g_tok.at[my_block]), here(cotangent, g_cot.at[my_block])]
    weight_copies = [
        here(w_in, wi.at[:, pl.ds(0, hid)]),
        here(w_out, wo.at[pl.ds(0, hid)]),
    ]

    barrier = pltpu.get_barrier_semaphore()
    friends = [x_partner, row_partner, core_partner] + list(along_y.values()) + list(along_z.values())
    for friend in friends:
        pl.semaphore_signal(barrier, inc=1, device_id=friend, device_id_type=MESH)
    pl.semaphore_wait(barrier, len(friends))

    def arrived(copies):
        for copy in copies:
            if id(copy) not in seen:
                seen.add(id(copy))
                copy.wait_recv()

    def landed(copy):
        if id(copy) not in seen:
            seen.add(id(copy))
            copy.wait()

    def half_of(kind):
        return low if kind == 0 else 1 - low

    def place(kind, di, j):
        h = half_of(kind)
        i0, j0 = y + h * (z - y), z + h * (y - z)
        return h, lax.rem(i0 + di, 4), piece(lax.rem(j0 + j, 4))

    def to_ring1(kind, o):
        h = half_of(kind)
        return at(dy=o * h, dz=o * (1 - h))

    def to_ring2(kind, o):
        h = half_of(kind)
        return at(dy=o * (1 - h), dz=o * h)

    own_src = {0: tokens, 1: cotangent}
    gathered = {0: g_tok, 1: g_cot}
    g0, one, two, three = {}, {}, {}, {}
    FORWARDS = ((0, 1), (1, 3), (3, 1), (2, 3))

    def send_x(k):
        g0[k] = remote(own_src[k], gathered[k].at[place(0, 0, 0)], x_partner)

    def source(k, kind, block):
        if kind == 0:
            return own_src[k]
        arrived([g0[k]])
        return block

    def ring1_send(k, kind):
        block = gathered[k].at[place(kind, 0, 0)]
        src = source(k, kind, block)
        one[k, kind] = {o: remote(src, block, to_ring1(kind, o)) for o in (1, 3)}

    def ring1_forward(k, kind):
        for o in (1, 3):
            arrived([one[k, kind][o]])
            h, i, r = place(kind, 0, 4 - o)
            block = gathered[k].at[h, i, r, pl.ds((o // 2) * (feat // 2), feat // 2)]
            one[k, kind, o] = remote(block, block, to_ring1(kind, o))

    def ring2_send(k, kind, j):
        block = gathered[k].at[place(kind, 0, j)]
        src = block
        if j == 0:
            src = source(k, kind, block)
        elif j == 2:
            arrived([one[k, kind, 1], one[k, kind, 3]])
        else:
            arrived([one[k, kind][4 - j]])
        two[k, kind, j] = {o: remote(src, block, to_ring2(kind, o)) for o in (1, 3)}

    def forward(k, kind, j, o):
        arrived([two[k, kind, j][o]])
        block = gathered[k].at[place(kind, 4 - o, j)]
        three[k, kind, j, o] = remote(block, block, to_ring2(kind, o))

    def gathered_side(k, o):
        for kind in range(2):
            for j in range(4):
                if (j, o) not in FORWARDS:
                    arrived([two[k, kind, j][o]])

    def gathered_far(k):
        for kind in range(2):
            for j, o in FORWARDS:
                arrived([three[k, kind, j, o]])

    for copy in own_copies:
        landed(copy)

    core, p, q = {}, {}, {}
    mine, other = pl.ds(0, hid), pl.ds(hid, hid)
    tile = feat // 3

    def send_weights():
        core["w_in"] = remote(w_in, wi.at[:, pl.ds(hid, hid)], core_partner)
        core["w_out"] = remote(w_out, wo.at[pl.ds(hid, hid)], core_partner)

    def rows_of(g, o):
        return jnp.concatenate([g[h, ring_at(h, o)] for h in range(2)], axis=0)

    def pre_step(s):
        landed(weight_copies[0])
        arrived([core["w_in"]])
        chunk = rows_of(g_tok, OFFSETS[s])
        p[s] = []
        for part in (mine, other):
            value = nn(chunk, wi[:, part])
            pre[s, :, part] = value
            s_pre[s, :, part] = value.astype(BF16)
            p[s].append(remote(s_pre.at[s, :, part], r_pre.at[s, :, part], row_partner))

    def dact_step(s):
        landed(weight_copies[1])
        arrived([core["w_out"]])
        chunk = rows_of(g_cot, OFFSETS[s])
        q[s] = []
        for part in (mine, other):
            value = nt(chunk, wo[part, :])
            dact[s, :, part] = value
            s_dact[s, :, part] = value.astype(BF16)
            q[s].append(remote(s_dact.at[s, :, part], r_dact.at[s, :, part], row_partner))

    def act_step(s):
        arrived(p[s])
        for h in range(2):
            i = ring_at(h, OFFSETS[s])

            def body(t, _):
                r_in = pl.ds(pl.multiple_of(h * slab + t * 16, 16), 16)
                r_out = pl.ds(pl.multiple_of(t * 16, 16), 16)
                hidden = pre[s, r_in, :] + r_pre[s, r_in, :].astype(F32)
                square = hidden * hidden
                inner = 0.7978845608 * (hidden + 0.044715 * square * hidden)
                tangent = jnp.tanh(inner)
                act[h, i, r_out, :] = (0.5 * hidden * (1.0 + tangent)).astype(BF16)
                pre[s, r_in, :] = 0.5 * (1.0 + tangent) + 0.5 * hidden * (
                    1.0 - tangent * tangent
                ) * 0.7978845608 * (1.0 + 3.0 * 0.044715 * square)
                return 0

            lax.fori_loop(0, slab // 16, body, 0)

    def dpre_step(s):
        arrived(q[s])
        for h in range(2):
            i = ring_at(h, OFFSETS[s])

            def body(t, _):
                r_in = pl.ds(pl.multiple_of(h * slab + t * 16, 16), 16)
                r_out = pl.ds(pl.multiple_of(t * 16, 16), 16)
                total = dact[s, r_in, :] + r_dact[s, r_in, :].astype(F32)
                dpre[h, i, r_out, :] = (total * pre[s, r_in, :]).astype(BF16)
                return 0

            lax.fori_loop(0, slab // 16, body, 0)

    low_rows, high_rows = slice(0, 2 * rows), slice(2 * rows, 4 * rows)

    def span(f):
        return pl.ds(f[0] * (feat // 6), f[1] * (feat // 6))

    def project(k, s, f):
        chunk = rows_of((act, dpre)[k], OFFSETS[s])
        o = OFFSETS[s]
        cols = span(f)
        landed(weight_copies[k - 1])
        arrived([core[("w_out", "w_in")[k]]])
        value = nn(chunk, wo[:, cols]) if k == 0 else nt(chunk, wi[cols, :])
        for h in range(2):
            part = value[h * slab:(h + 1) * slab]
            if o == 2:
                q2[k, h, :, cols] = part.astype(BF16)
            elif o == 1:
                s1[k, h, 0, high_rows, cols] = part[high_rows].astype(BF16)
                mid[k, h, 0, :, cols] = part[low_rows]
            elif o == 3:
                s1[k, h, 1, low_rows, cols] = part[low_rows].astype(BF16)
                mid[k, h, 1, :, cols] = part[high_rows]
            else:
                acc[k, h, :, cols] = part

    whole, first, last = (0, 6), (0, 4), (4, 2)
    far, near, merged, second, third = {}, {}, {}, {}, {}

    def scatter_far(k, f):
        project(k, 3, f)
        cols = span(f)
        far[k, f] = []
        for h in range(2):
            for side, part in enumerate((low_rows, high_rows)):
                far[k, f].append(remote(
                    q2.at[k, h, part, cols], r2.at[k, h, side, :, cols], ring2[h][(1, 3)[side]]
                ))

    def scatter_near(k, f, side):
        project(k, 1 + side, f)
        part = (high_rows, low_rows)[side]
        cols = span(f)
        near.setdefault((k, f), []).extend(
            remote(s1.at[k, h, side, part, cols], r1.at[k, h, side, part, cols], ring2[h][(1, 3)[side]])
            for h in range(2)
        )

    def scatter_merge(k, f):
        cols = span(f)
        merged[k, f] = []
        for h in range(2):
            for side in range(2):
                arrived([far[k, f][2 * h + side]])
                base = side * 2 * rows

                def body(t, _):
                    r_in = pl.ds(pl.multiple_of(t * 16, 16), 16)
                    r_out = pl.ds(pl.multiple_of(base + t * 16, 16), 16)
                    total = mid[k, h, side, r_in, cols] + r2[k, h, side, r_in, cols].astype(F32)
                    s1[k, h, side, r_out, cols] = total.astype(BF16)
                    return 0

                lax.fori_loop(0, 2 * rows // 16, body, 0)
                part = (low_rows, high_rows)[side]
                merged[k, f].append(remote(
                    s1.at[k, h, side, part, cols], r1.at[k, h, side, part, cols],
                    ring2[h][(1, 3)[side]],
                ))

    def scatter_two(k, f):
        cols = span(f)
        arrived(near[k, f])
        arrived(merged[k, f])
        second[k, f] = []
        for h in range(2):
            for slot, o in enumerate((2, 1, 3)):
                r_in = piece(lax.rem(sub[h] + o, 4))
                total = acc[k, h, r_in, cols] + r1[k, h, 0, r_in, cols].astype(F32)
                u2[k, h, slot, :, cols] = (total + r1[k, h, 1, r_in, cols].astype(F32)).astype(BF16)
                second[k, f].append(remote(
                    u2.at[k, h, slot, :, cols], v2.at[k, h, slot, :, cols], ring1[h][o]
                ))

    left_cols, right_cols = pl.ds(0, feat // 2), pl.ds(feat // 2, feat // 2)

    def term(k, h, o, cols):
        r_in = piece(lax.rem(sub[h] + o, 4))
        total = acc[k, h, r_in, cols] + r1[k, h, 0, r_in, cols].astype(F32)
        return total + r1[k, h, 1, r_in, cols].astype(F32)

    def second_send(k, h, slot, cols, o):
        return remote(u2.at[k, h, slot, :, cols], v2.at[k, h, slot, :, cols], ring1[h][o])

    def scatter_two_start(k):
        arrived(near[k, whole])
        arrived(merged[k, whole])
        second[k, whole] = []
        for h in range(2):
            for cols, o in ((left_cols, 1), (right_cols, 3)):
                u2[k, h, 0, :, cols] = term(k, h, 2, cols).astype(BF16)
                second[k, whole].append(second_send(k, h, 0, cols, o))
            u2[k, h, 1, :, right_cols] = term(k, h, 1, right_cols).astype(BF16)
            second[k, whole].append(second_send(k, h, 1, right_cols, 1))
            u2[k, h, 2, :, left_cols] = term(k, h, 3, left_cols).astype(BF16)
            second[k, whole].append(second_send(k, h, 2, left_cols, 3))

    def scatter_two_merge(k):
        for h in range(2):
            for cols, o, slot in ((left_cols, 1, 1), (right_cols, 3, 2)):
                arrived([second[k, whole][4 * h + slot - 1]])
                total = term(k, h, o, cols) + v2[k, h, 0, :, cols].astype(F32)
                u2[k, h, slot, :, cols] = total.astype(BF16)
                second[k, whole].append(second_send(k, h, slot, cols, o))

    def scatter_three(k, f):
        cols = span(f)
        arrived(second[k, f])
        for h in range(2):
            r_in = piece(sub[h])
            total = acc[k, h, r_in, cols] + r1[k, h, 0, r_in, cols].astype(F32)
            total += r1[k, h, 1, r_in, cols].astype(F32)
            for slot in range(1 - k, 3):
                total += v2[k, h, slot, :, cols].astype(F32)
            fin[k, h, :, cols] = total
        s3[k, :, cols] = fin[k, 1 - low, :, cols].astype(BF16)
        third[k, f] = remote(s3.at[k, :, cols], r3.at[k, :, cols], x_partner)

    def finish(k, f):
        cols = span(f)
        arrived([third[k, f]])
        (out, gin)[k][:, cols] = (fin[k, low, :, cols] + r3[k, :, cols].astype(F32)).astype(BF16)

    tokens_all = 8 * slab

    def flat(value):
        return value.reshape(tokens_all, value.shape[-1])

    def send_core(name):
        src, dst = {
            "tok": (g_tok, e_tok),
            "cot": (g_cot, e_cot),
            "act": (act.at[:, :, :, other], e_act),
            "dpre": (dpre.at[:, :, :, other], e_dpre),
        }[name]
        core[name] = remote(src, dst, core_partner)

    def turn_act():
        arrived([core["act"]])
        act_t[0] = jnp.transpose(flat(act[:, :, :, mine]))
        act_t[1] = jnp.transpose(flat(e_act[...]))

    def grad_out_part(start, stop):
        arrived([core["cot"]])

        def body(t, _):
            cols = pl.ds(pl.multiple_of(t * tile, tile), tile)
            value = nn(act_t[0], flat(g_cot[:, :, :, cols]))
            grad_out[:, cols] = value + nn(act_t[1], flat(e_cot[:, :, :, cols]))
            return 0

        lax.fori_loop(start, stop, body, 0)

    def grad_in_part(start, stop):
        arrived([core["tok"], core["dpre"]])

        def body(t, _):
            cols = pl.ds(pl.multiple_of(t * tile, tile), tile)
            value = contract_rows(flat(g_tok[:, :, :, cols]), flat(dpre[:, :, :, mine]))
            value += contract_rows(flat(e_tok[:, :, :, cols]), flat(e_dpre[...]))
            grad_in[cols, :] = value
            return 0

        lax.fori_loop(start, stop, body, 0)

    send_x(0)
    ring1_send(0, 0)
    ring2_send(0, 0, 0)
    ring1_send(1, 0)
    send_weights()
    ring2_send(1, 0, 0)
    ring1_send(0, 1)
    ring1_forward(0, 0)
    ring2_send(0, 1, 0)
    ring2_send(0, 0, 1)
    send_x(1)
    ring1_forward(1, 0)
    ring1_forward(0, 1)
    ring2_send(0, 0, 3)
    ring2_send(0, 1, 1)
    ring2_send(0, 0, 2)
    ring2_send(0, 1, 3)
    forward(0, 0, 0, 1)
    ring1_send(1, 1)
    ring2_send(0, 1, 2)
    forward(0, 0, 1, 3)
    pre_step(0)
    forward(0, 1, 0, 1)
    forward(0, 1, 1, 3)
    forward(0, 0, 3, 1)
    forward(0, 1, 3, 1)
    gathered_side(0, 1)
    forward(0, 1, 2, 3)
    forward(0, 0, 2, 3)
    ring2_send(1, 1, 0)
    gathered_side(0, 3)
    ring2_send(1, 0, 1)
    pre_step(2)
    ring2_send(1, 1, 3)
    ring2_send(1, 1, 1)
    ring1_forward(1, 1)
    ring2_send(1, 0, 2)
    gathered_far(0)
    pre_step(3)
    pre_step(1)
    ring2_send(1, 0, 3)
    ring2_send(1, 1, 2)
    send_core("tok")
    forward(1, 0, 1, 3)
    forward(1, 0, 0, 1)
    act_step(0)
    forward(1, 1, 1, 3)
    act_step(2)
    forward(1, 1, 0, 1)
    forward(1, 1, 3, 1)
    project(0, 0, whole)
    forward(1, 1, 2, 3)
    forward(1, 0, 2, 3)
    forward(1, 0, 3, 1)
    act_step(3)
    scatter_far(0, whole)
    gathered_side(1, 3)
    gathered_side(1, 1)
    dact_step(1)
    scatter_near(0, whole, 1)
    gathered_far(1)
    act_step(1)
    scatter_near(0, whole, 0)
    dact_step(3)
    send_core("act")
    dact_step(2)
    send_core("cot")
    scatter_merge(0, whole)
    dact_step(0)
    dpre_step(1)
    scatter_near(1, last, 0)
    dpre_step(3)
    scatter_far(1, last)
    scatter_far(1, first)
    scatter_near(1, first, 0)
    scatter_two_start(0)
    dpre_step(2)
    scatter_near(1, last, 1)
    scatter_near(1, first, 1)
    scatter_merge(1, first)
    dpre_step(0)
    send_core("dpre")
    scatter_merge(1, last)
    project(1, 0, whole)
    turn_act()
    scatter_two_merge(0)
    grad_out_part(0, 1)
    scatter_two(1, first)
    grad_in_part(1, 2)
    scatter_two(1, last)
    scatter_three(0, whole)
    grad_out_part(1, 2)
    grad_in_part(2, 3)
    scatter_three(1, first)
    grad_out_part(2, 3)
    scatter_three(1, last)
    grad_in_part(0, 1)
    finish(1, first)
    finish(0, whole)
    finish(1, last)
    for copy in sent:
        copy.wait_send()


def exchange(tokens_in, w_in, w_out, grad_output):
    rows, feat = tokens_in.shape
    hid = w_in.shape[1]
    slab = 4 * rows
    vmem, hbm = pl.BlockSpec(memory_space=pltpu.VMEM), pl.BlockSpec(memory_space=pl.ANY)
    scratch = [
        ((2, 4, slab, feat), BF16),
        ((2, 4, slab, feat), BF16),
        ((2, 4, slab, feat), BF16),
        ((2, 4, slab, feat), BF16),
        ((2, 4, slab, hid), BF16),
        ((2, 4, slab, hid), BF16),
        ((2, hid, 8 * slab), BF16),
        ((feat, 2 * hid), BF16),
        ((2 * hid, feat), BF16),
        ((4, 2 * slab, 2 * hid), F32),
        ((4, 2 * slab, 2 * hid), F32),
        ((4, 2 * slab, 2 * hid), BF16),
        ((4, 2 * slab, 2 * hid), BF16),
        ((4, 2 * slab, 2 * hid), BF16),
        ((4, 2 * slab, 2 * hid), BF16),
        ((2, 4, slab, 2 * hid), BF16),
        ((2, 4, slab, 2 * hid), BF16),
        ((2, 2, slab, feat), BF16),
        ((2, 2, 2, 2 * rows, feat), BF16),
        ((2, 2, 2, 2 * rows, feat), F32),
        ((2, 2, 2, slab, feat), BF16),
        ((2, 2, 2, slab, feat), BF16),
        ((2, 2, slab, feat), F32),
        ((2, 2, 3, rows, feat), BF16),
        ((2, 2, 3, rows, feat), BF16),
        ((2, 2, rows, feat), F32),
        ((2, rows, feat), BF16),
        ((2, rows, feat), BF16),
    ]
    return pl.pallas_call(
        kernel,
        out_shape=[
            pltpu.VMEM((rows, feat), BF16),
            pltpu.VMEM((rows, feat), BF16),
            pltpu.VMEM((feat, hid), F32),
            pltpu.VMEM((hid, feat), F32),
        ],
        in_specs=[hbm] * 4,
        out_specs=[vmem] * 4,
        scratch_shapes=[pltpu.VMEM(*s) for s in scratch] + [
            pltpu.SemaphoreType.DMA((N_REMOTE,)),
            pltpu.SemaphoreType.DMA((N_REMOTE,)),
            pltpu.SemaphoreType.DMA((N_LOCAL,)),
        ],
        compiler_params=pltpu.CompilerParams(
            collective_id=0, has_side_effects=True, vmem_limit_bytes=52 * 2**20
        ),
        name="exchange",
    )(tokens_in, w_in, w_out, grad_output)


def drain_kernel(*refs):
    n = len(refs) // 2
    copies = [pltpu.make_async_copy(refs[i], refs[n + i], refs[-1].at[i]) for i in range(n)]
    for copy in copies:
        copy.start()
    for copy in copies:
        copy.wait()


def drain(arrays):
    arrays = [pltpu.with_memory_space_constraint(a, pltpu.VMEM) for a in arrays]
    anywhere = [pl.BlockSpec(memory_space=pl.ANY)] * len(arrays)
    return pl.pallas_call(
        drain_kernel,
        out_shape=[pltpu.HBM(a.shape, a.dtype) for a in arrays],
        in_specs=anywhere,
        out_specs=anywhere,
        scratch_shapes=[pltpu.SemaphoreType.DMA((len(arrays),))],
        compiler_params=pltpu.CompilerParams(vmem_limit_bytes=2**20),
        name="drain",
    )(*arrays)


def per_device(*arrays):
    return tuple(drain(exchange(*arrays)))


def solution(mesh):
    placed = (
        P(("depth", "col"), "row"),
        P("row", ("depth", "col")),
        P(("depth", "col"), "row"),
        P(("depth", "col"), "row"),
    )
    return jax.shard_map(
        per_device,
        mesh=mesh,
        in_specs=placed,
        out_specs=(
            P(("depth", "col"), "row"),
            P(("depth", "col"), "row"),
            P("row", ("depth", "col")),
            P(("depth", "col"), "row"),
        ),
        check_vma=False,
    )
```

```python
import functools

import jax
import jax.numpy as jnp
from jax import lax
from jax.experimental import pallas as pl
from jax.experimental.pallas import tpu as pltpu
from jax.sharding import PartitionSpec as P

MESH = pl.DeviceIdType.MESH
BF16, F32 = jnp.bfloat16, jnp.float32
OFFSETS = (0, 1, 3, 2)
N_REMOTE = 208
N_LOCAL = 16


def contract_rows(left, right):
    return lax.dot_general(left, right, (((0,), (0,)), ((), ())), preferred_element_type=F32)


def nn(left, right):
    return jnp.dot(left, right, preferred_element_type=F32)


def nt(left, right):
    return lax.dot_general(left, right, (((1,), (1,)), ((), ())), preferred_element_type=F32)


def kernel(
    tokens, w_in, w_out, cotangent,
    out, gin, grad_in, grad_out,
    g_tok, g_cot, e_tok, e_cot, e_act, e_dpre, act_t, wi, wo, pre, dact, s_pre, r_pre, s_dact, r_dact, act, dpre,
    q2, r2, mid, s1, r1, acc, u2, v2, fin, s3, r3,
    send, recv, local,
):
    rows, feat = tokens.shape
    hid = w_in.shape[1]
    slab = 4 * rows
    depth, row, col = lax.axis_index("depth"), lax.axis_index("row"), lax.axis_index("col")
    low = lax.rem(col, 2)
    y = lax.rem(lax.div(col, 2), 4)
    z = lax.div(col, 8)

    def at(dy=0, dz=0, lo=None, r=None, d=None):
        c = lax.rem(z + dz, 4) * 8 + lax.rem(y + dy, 4) * 2 + (low if lo is None else lo)
        return (depth if d is None else d, row if r is None else r, c)

    x_partner = at(lo=1 - low)
    row_partner = at(r=1 - row)
    core_partner = at(d=1 - depth)
    along_y = {o: at(dy=o) for o in (1, 2, 3)}
    along_z = {o: at(dz=o) for o in (1, 2, 3)}
    ring1 = (along_z, along_y)
    ring2 = (along_y, along_z)
    own = (y, z)
    sub = (z, y)

    counter, counter_local, sent, seen = [0], [0], [], set()

    def remote(src, dst, device):
        i = counter[0]
        counter[0] += 1
        copy = pltpu.make_async_remote_copy(
            src_ref=src, dst_ref=dst, send_sem=send.at[i], recv_sem=recv.at[i],
            device_id=device, device_id_type=MESH,
        )
        copy.start()
        sent.append(copy)
        return copy

    def here(src, dst):
        i = counter_local[0]
        counter_local[0] += 1
        copy = pltpu.make_async_copy(src, dst, local.at[i])
        copy.start()
        return copy

    def piece(j):
        return pl.ds(pl.multiple_of(j * rows, rows), rows)

    def ring_at(h, o):
        return lax.rem(own[h] + o, 4)

    my_block = (low, y + low * (z - y), piece(z + low * (y - z)))
    own_copies = [here(tokens, g_tok.at[my_block]), here(cotangent, g_cot.at[my_block])]
    weight_copies = [
        here(w_in, wi.at[:, pl.ds(0, hid)]),
        here(w_out, wo.at[pl.ds(0, hid)]),
    ]

    barrier = pltpu.get_barrier_semaphore()
    friends = [x_partner, row_partner, core_partner] + list(along_y.values()) + list(along_z.values())
    for friend in friends:
        pl.semaphore_signal(barrier, inc=1, device_id=friend, device_id_type=MESH)
    pl.semaphore_wait(barrier, len(friends))

    def arrived(copies):
        for copy in copies:
            if id(copy) not in seen:
                seen.add(id(copy))
                copy.wait_recv()

    def landed(copy):
        if id(copy) not in seen:
            seen.add(id(copy))
            copy.wait()

    def half_of(kind):
        return low if kind == 0 else 1 - low

    def place(kind, di, j):
        h = half_of(kind)
        i0, j0 = y + h * (z - y), z + h * (y - z)
        return h, lax.rem(i0 + di, 4), piece(lax.rem(j0 + j, 4))

    def to_ring1(kind, o):
        h = half_of(kind)
        return at(dy=o * h, dz=o * (1 - h))

    def to_ring2(kind, o):
        h = half_of(kind)
        return at(dy=o * (1 - h), dz=o * h)

    own_src = {0: tokens, 1: cotangent}
    gathered = {0: g_tok, 1: g_cot}
    g0, one, two, three, swapped = {}, {}, {}, {}, {}
    FORWARDS = ((0, 1), (1, 3), (3, 1), (2, 3))

    def send_x(k):
        g0[k] = remote(own_src[k], gathered[k].at[place(0, 0, 0)], x_partner)

    def source(k, kind, block):
        if kind == 0:
            return own_src[k]
        arrived([g0[k]])
        return block

    def columns(k, kind):
        return (0, feat) if k == 0 else (kind * (feat // 2), feat // 2)

    def ring1_send(k, kind):
        block = gathered[k].at[place(kind, 0, 0)]
        src = source(k, kind, block)
        start, size = columns(k, kind)
        cols = pl.ds(start, size)
        one[k, kind] = {
            o: remote(src.at[:, cols], block.at[:, cols], to_ring1(kind, o)) for o in (1, 3)
        }

    def ring1_forward(k, kind):
        for o in (1, 3):
            arrived([one[k, kind][o]])
            h, i, r = place(kind, 0, 4 - o)
            start, size = columns(k, kind)
            block = gathered[k].at[h, i, r, pl.ds(start + (o // 2) * (size // 2), size // 2)]
            one[k, kind, o] = remote(block, block, to_ring1(kind, o))

    def swap(kind, j):
        arrived([one[1, kind, 1], one[1, kind, 3]] if j == 2 else [one[1, kind][4 - j]])
        h, i, r = place(kind, 0, j)
        start, size = columns(1, kind)
        block = g_cot.at[h, i, r, pl.ds(start, size)]
        swapped[kind, j] = remote(block, block, x_partner)

    def ring2_send(k, kind, j):
        block = gathered[k].at[place(kind, 0, j)]
        src = block
        if j == 0:
            src = source(k, kind, block)
        elif j == 2:
            arrived([one[k, kind, 1], one[k, kind, 3]])
        else:
            arrived([one[k, kind][4 - j]])
        if k == 1 and j > 0:
            arrived([swapped[1 - kind, j]])
        two[k, kind, j] = {o: remote(src, block, to_ring2(kind, o)) for o in (1, 3)}

    def forward(k, kind, j, o):
        arrived([two[k, kind, j][o]])
        block = gathered[k].at[place(kind, 4 - o, j)]
        three[k, kind, j, o] = remote(block, block, to_ring2(kind, o))

    def gathered_side(k, o):
        for kind in range(2):
            for j in range(4):
                if (j, o) not in FORWARDS:
                    arrived([two[k, kind, j][o]])

    def gathered_far(k):
        for kind in range(2):
            for j, o in FORWARDS:
                arrived([three[k, kind, j, o]])

    for copy in own_copies:
        landed(copy)

    core, p, q = {}, {}, {}
    mine, other = pl.ds(0, hid), pl.ds(hid, hid)
    tile = feat // 3

    def send_weights():
        core["w_in"] = remote(w_in, wi.at[:, pl.ds(hid, hid)], core_partner)
        core["w_out"] = remote(w_out, wo.at[pl.ds(hid, hid)], core_partner)

    def rows_of(g, o):
        return jnp.concatenate([g[h, ring_at(h, o)] for h in range(2)], axis=0)

    def pre_step(s):
        landed(weight_copies[0])
        arrived([core["w_in"]])
        chunk = rows_of(g_tok, OFFSETS[s])
        p[s] = []
        for part in (mine, other):
            value = nn(chunk, wi[:, part])
            pre[s, :, part] = value
            s_pre[s, :, part] = value.astype(BF16)
            p[s].append(remote(s_pre.at[s, :, part], r_pre.at[s, :, part], row_partner))

    def dact_step(s):
        landed(weight_copies[1])
        arrived([core["w_out"]])
        chunk = rows_of(g_cot, OFFSETS[s])
        q[s] = []
        for part in (mine, other):
            value = nt(chunk, wo[part, :])
            dact[s, :, part] = value
            s_dact[s, :, part] = value.astype(BF16)
            q[s].append(remote(s_dact.at[s, :, part], r_dact.at[s, :, part], row_partner))

    def act_step(s):
        arrived(p[s])
        for h in range(2):
            i = ring_at(h, OFFSETS[s])

            def body(t, _):
                r_in = pl.ds(pl.multiple_of(h * slab + t * 16, 16), 16)
                r_out = pl.ds(pl.multiple_of(t * 16, 16), 16)
                hidden = pre[s, r_in, :] + r_pre[s, r_in, :].astype(F32)
                square = hidden * hidden
                inner = 0.7978845608 * (hidden + 0.044715 * square * hidden)
                tangent = jnp.tanh(inner)
                act[h, i, r_out, :] = (0.5 * hidden * (1.0 + tangent)).astype(BF16)
                pre[s, r_in, :] = 0.5 * (1.0 + tangent) + 0.5 * hidden * (
                    1.0 - tangent * tangent
                ) * 0.7978845608 * (1.0 + 3.0 * 0.044715 * square)
                return 0

            lax.fori_loop(0, slab // 16, body, 0)

    def dpre_step(s):
        arrived(q[s])
        for h in range(2):
            i = ring_at(h, OFFSETS[s])

            def body(t, _):
                r_in = pl.ds(pl.multiple_of(h * slab + t * 16, 16), 16)
                r_out = pl.ds(pl.multiple_of(t * 16, 16), 16)
                total = dact[s, r_in, :] + r_dact[s, r_in, :].astype(F32)
                dpre[h, i, r_out, :] = (total * pre[s, r_in, :]).astype(BF16)
                return 0

            lax.fori_loop(0, slab // 16, body, 0)

    low_rows, high_rows = slice(0, 2 * rows), slice(2 * rows, 4 * rows)

    def span(f):
        return pl.ds(f[0] * (feat // 6), f[1] * (feat // 6))

    def project(k, s, f):
        chunk = rows_of((act, dpre)[k], OFFSETS[s])
        o = OFFSETS[s]
        cols = span(f)
        landed(weight_copies[k - 1])
        arrived([core[("w_out", "w_in")[k]]])
        value = nn(chunk, wo[:, cols]) if k == 0 else nt(chunk, wi[cols, :])
        for h in range(2):
            part = value[h * slab:(h + 1) * slab]
            if o == 2:
                q2[k, h, :, cols] = part.astype(BF16)
            elif o == 1:
                s1[k, h, 0, high_rows, cols] = part[high_rows].astype(BF16)
                mid[k, h, 0, :, cols] = part[low_rows]
            elif o == 3:
                s1[k, h, 1, low_rows, cols] = part[low_rows].astype(BF16)
                mid[k, h, 1, :, cols] = part[high_rows]
            else:
                acc[k, h, :, cols] = part

    whole = (0, 6)
    far, near, merged, second, third = {}, {}, {}, {}, {}

    def scatter_far(k, f):
        project(k, 3, f)
        cols = span(f)
        far[k, f] = []
        for h in range(2):
            for side, part in enumerate((low_rows, high_rows)):
                far[k, f].append(remote(
                    q2.at[k, h, part, cols], r2.at[k, h, side, :, cols], ring2[h][(1, 3)[side]]
                ))

    def scatter_near(k, f, side):
        project(k, 1 + side, f)
        part = (high_rows, low_rows)[side]
        cols = span(f)
        near.setdefault((k, f), []).extend(
            remote(s1.at[k, h, side, part, cols], r1.at[k, h, side, part, cols], ring2[h][(1, 3)[side]])
            for h in range(2)
        )

    def scatter_merge(k, f):
        cols = span(f)
        merged[k, f] = []
        for h in range(2):
            for side in range(2):
                arrived([far[k, f][2 * h + side]])
                base = side * 2 * rows

                def body(t, _):
                    r_in = pl.ds(pl.multiple_of(t * 16, 16), 16)
                    r_out = pl.ds(pl.multiple_of(base + t * 16, 16), 16)
                    total = mid[k, h, side, r_in, cols] + r2[k, h, side, r_in, cols].astype(F32)
                    s1[k, h, side, r_out, cols] = total.astype(BF16)
                    return 0

                lax.fori_loop(0, 2 * rows // 16, body, 0)
                part = (low_rows, high_rows)[side]
                merged[k, f].append(remote(
                    s1.at[k, h, side, part, cols], r1.at[k, h, side, part, cols],
                    ring2[h][(1, 3)[side]],
                ))

    def scatter_two(k, f):
        cols = span(f)
        arrived(near[k, f])
        arrived(merged[k, f])
        second[k, f] = []
        for h in range(2):
            for slot, o in enumerate((2, 1, 3)):
                r_in = piece(lax.rem(sub[h] + o, 4))
                total = acc[k, h, r_in, cols] + r1[k, h, 0, r_in, cols].astype(F32)
                u2[k, h, slot, :, cols] = (total + r1[k, h, 1, r_in, cols].astype(F32)).astype(BF16)
                second[k, f].append(remote(
                    u2.at[k, h, slot, :, cols], v2.at[k, h, slot, :, cols], ring1[h][o]
                ))

    left_cols, right_cols = pl.ds(0, feat // 2), pl.ds(feat // 2, feat // 2)

    def term(k, h, o, cols):
        r_in = piece(lax.rem(sub[h] + o, 4))
        total = acc[k, h, r_in, cols] + r1[k, h, 0, r_in, cols].astype(F32)
        return total + r1[k, h, 1, r_in, cols].astype(F32)

    def second_send(k, h, slot, cols, o):
        return remote(u2.at[k, h, slot, :, cols], v2.at[k, h, slot, :, cols], ring1[h][o])

    def scatter_two_start(k):
        arrived(near[k, whole])
        arrived(merged[k, whole])
        second[k, whole] = []
        for h in range(2):
            for cols, o in ((left_cols, 1), (right_cols, 3)):
                u2[k, h, 0, :, cols] = term(k, h, 2, cols).astype(BF16)
                second[k, whole].append(second_send(k, h, 0, cols, o))
            u2[k, h, 1, :, right_cols] = term(k, h, 1, right_cols).astype(BF16)
            second[k, whole].append(second_send(k, h, 1, right_cols, 1))
            u2[k, h, 2, :, left_cols] = term(k, h, 3, left_cols).astype(BF16)
            second[k, whole].append(second_send(k, h, 2, left_cols, 3))

    def scatter_two_merge(k):
        for h in range(2):
            for cols, o, slot in ((left_cols, 1, 1), (right_cols, 3, 2)):
                arrived([second[k, whole][4 * h + slot - 1]])
                total = term(k, h, o, cols) + v2[k, h, 0, :, cols].astype(F32)
                u2[k, h, slot, :, cols] = total.astype(BF16)
                second[k, whole].append(second_send(k, h, slot, cols, o))

    def scatter_three(k, f):
        cols = span(f)
        arrived(second[k, f])
        for h in range(2):
            r_in = piece(sub[h])
            total = acc[k, h, r_in, cols] + r1[k, h, 0, r_in, cols].astype(F32)
            total += r1[k, h, 1, r_in, cols].astype(F32)
            for slot in range(1 - k, 3):
                total += v2[k, h, slot, :, cols].astype(F32)
            fin[k, h, :, cols] = total
        s3[k, :, cols] = fin[k, 1 - low, :, cols].astype(BF16)
        third[k, f] = remote(s3.at[k, :, cols], r3.at[k, :, cols], x_partner)

    def finish(k, f):
        cols = span(f)
        arrived([third[k, f]])
        (out, gin)[k][:, cols] = (fin[k, low, :, cols] + r3[k, :, cols].astype(F32)).astype(BF16)

    tokens_all = 8 * slab

    def flat(value):
        return value.reshape(tokens_all, value.shape[-1])

    def send_core(name):
        src, dst = {
            "tok": (g_tok, e_tok),
            "cot": (g_cot, e_cot),
            "act": (act.at[:, :, :, other], e_act),
            "dpre": (dpre.at[:, :, :, other], e_dpre),
        }[name]
        core[name] = remote(src, dst, core_partner)

    def turn_act():
        arrived([core["act"]])
        act_t[0] = jnp.transpose(flat(act[:, :, :, mine]))
        act_t[1] = jnp.transpose(flat(e_act[...]))

    def grad_out_part(start, stop):
        arrived([core["cot"]])

        def body(t, _):
            cols = pl.ds(pl.multiple_of(t * tile, tile), tile)
            value = nn(act_t[0], flat(g_cot[:, :, :, cols]))
            grad_out[:, cols] = value + nn(act_t[1], flat(e_cot[:, :, :, cols]))
            return 0

        lax.fori_loop(start, stop, body, 0)

    def grad_in_part(start, stop):
        arrived([core["tok"], core["dpre"]])

        def body(t, _):
            cols = pl.ds(pl.multiple_of(t * tile, tile), tile)
            value = contract_rows(flat(g_tok[:, :, :, cols]), flat(dpre[:, :, :, mine]))
            value += contract_rows(flat(e_tok[:, :, :, cols]), flat(e_dpre[...]))
            grad_in[cols, :] = value
            return 0

        lax.fori_loop(start, stop, body, 0)

    send_x(0)
    send_weights()
    ring2_send(0, 0, 0)
    ring1_send(1, 0)
    ring1_send(0, 0)
    ring2_send(1, 0, 0)
    send_x(1)
    ring1_forward(1, 0)
    swap(0, 1)
    ring2_send(0, 1, 0)
    swap(0, 3)
    ring1_send(0, 1)
    ring1_forward(0, 0)
    swap(0, 2)
    ring1_send(1, 1)
    ring2_send(1, 1, 0)
    ring2_send(0, 0, 1)
    ring2_send(0, 1, 1)
    ring1_forward(0, 1)
    ring2_send(0, 1, 3)
    swap(1, 1)
    forward(0, 1, 0, 1)
    ring1_forward(1, 1)
    ring2_send(0, 0, 3)
    swap(1, 3)
    forward(0, 0, 0, 1)
    ring2_send(0, 0, 2)
    swap(1, 2)
    ring2_send(0, 1, 2)
    pre_step(0)
    forward(0, 1, 1, 3)
    forward(0, 1, 3, 1)
    forward(0, 0, 1, 3)
    forward(0, 0, 3, 1)
    forward(0, 0, 2, 3)
    forward(0, 1, 2, 3)
    ring2_send(1, 0, 1)
    ring2_send(1, 1, 1)
    ring2_send(1, 0, 3)
    ring2_send(1, 1, 3)
    gathered_side(0, 3)
    ring2_send(1, 1, 2)
    pre_step(1)
    act_step(0)
    gathered_far(0)
    pre_step(3)
    ring2_send(1, 0, 2)
    gathered_side(0, 1)
    forward(1, 0, 0, 1)
    pre_step(2)
    forward(1, 1, 0, 1)
    project(0, 0, whole)
    forward(1, 0, 1, 3)
    forward(1, 1, 1, 3)
    send_core("tok")
    forward(1, 1, 3, 1)
    forward(1, 0, 3, 1)
    forward(1, 0, 2, 3)
    gathered_side(1, 1)
    forward(1, 1, 2, 3)
    act_step(1)
    act_step(3)
    scatter_far(0, whole)
    gathered_side(1, 3)
    dact_step(2)
    gathered_far(1)
    scatter_near(0, whole, 0)
    act_step(2)
    scatter_near(0, whole, 1)
    dact_step(3)
    send_core("cot")
    scatter_merge(0, whole)
    dact_step(1)
    dpre_step(2)
    dact_step(0)
    scatter_near(1, (3, 2), 1)
    dpre_step(3)
    scatter_far(1, (5, 1))
    scatter_far(1, (3, 2))
    scatter_near(1, (5, 1), 1)
    scatter_far(1, (0, 3))
    scatter_two_start(0)
    scatter_near(1, (0, 3), 1)
    dpre_step(1)
    scatter_near(1, (0, 3), 0)
    send_core("act")
    scatter_near(1, (3, 2), 0)
    dpre_step(0)
    scatter_merge(1, (0, 3))
    send_core("dpre")
    scatter_near(1, (5, 1), 0)
    scatter_two_merge(0)
    scatter_merge(1, (3, 2))
    scatter_merge(1, (5, 1))
    turn_act()
    project(1, 0, whole)
    grad_out_part(1, 2)
    scatter_two(1, (0, 3))
    grad_in_part(2, 3)
    scatter_three(0, whole)
    grad_out_part(2, 3)
    scatter_two(1, (3, 2))
    scatter_two(1, (5, 1))
    grad_out_part(0, 1)
    grad_in_part(0, 1)
    scatter_three(1, (0, 3))
    finish(0, whole)
    scatter_three(1, (3, 2))
    scatter_three(1, (5, 1))
    grad_in_part(1, 2)
    finish(1, (0, 3))
    finish(1, (3, 2))
    finish(1, (5, 1))
    for copy in sent:
        copy.wait_send()


def exchange(tokens_in, w_in, w_out, grad_output):
    rows, feat = tokens_in.shape
    hid = w_in.shape[1]
    slab = 4 * rows
    vmem, hbm = pl.BlockSpec(memory_space=pltpu.VMEM), pl.BlockSpec(memory_space=pl.ANY)
    scratch = [
        ((2, 4, slab, feat), BF16),
        ((2, 4, slab, feat), BF16),
        ((2, 4, slab, feat), BF16),
        ((2, 4, slab, feat), BF16),
        ((2, 4, slab, hid), BF16),
        ((2, 4, slab, hid), BF16),
        ((2, hid, 8 * slab), BF16),
        ((feat, 2 * hid), BF16),
        ((2 * hid, feat), BF16),
        ((4, 2 * slab, 2 * hid), F32),
        ((4, 2 * slab, 2 * hid), F32),
        ((4, 2 * slab, 2 * hid), BF16),
        ((4, 2 * slab, 2 * hid), BF16),
        ((4, 2 * slab, 2 * hid), BF16),
        ((4, 2 * slab, 2 * hid), BF16),
        ((2, 4, slab, 2 * hid), BF16),
        ((2, 4, slab, 2 * hid), BF16),
        ((2, 2, slab, feat), BF16),
        ((2, 2, 2, 2 * rows, feat), BF16),
        ((2, 2, 2, 2 * rows, feat), F32),
        ((2, 2, 2, slab, feat), BF16),
        ((2, 2, 2, slab, feat), BF16),
        ((2, 2, slab, feat), F32),
        ((2, 2, 3, rows, feat), BF16),
        ((2, 2, 3, rows, feat), BF16),
        ((2, 2, rows, feat), F32),
        ((2, rows, feat), BF16),
        ((2, rows, feat), BF16),
    ]
    return pl.pallas_call(
        kernel,
        out_shape=[
            pltpu.VMEM((rows, feat), BF16),
            pltpu.VMEM((rows, feat), BF16),
            pltpu.VMEM((feat, hid), F32),
            pltpu.VMEM((hid, feat), F32),
        ],
        in_specs=[hbm] * 4,
        out_specs=[vmem] * 4,
        scratch_shapes=[pltpu.VMEM(*s) for s in scratch] + [
            pltpu.SemaphoreType.DMA((N_REMOTE,)),
            pltpu.SemaphoreType.DMA((N_REMOTE,)),
            pltpu.SemaphoreType.DMA((N_LOCAL,)),
        ],
        compiler_params=pltpu.CompilerParams(
            collective_id=0, has_side_effects=True, vmem_limit_bytes=52 * 2**20
        ),
        name="exchange",
    )(tokens_in, w_in, w_out, grad_output)


def drain_kernel(*refs):
    n = len(refs) // 2
    copies = [pltpu.make_async_copy(refs[i], refs[n + i], refs[-1].at[i]) for i in range(n)]
    for copy in copies:
        copy.start()
    for copy in copies:
        copy.wait()


def drain(arrays):
    arrays = [pltpu.with_memory_space_constraint(a, pltpu.VMEM) for a in arrays]
    anywhere = [pl.BlockSpec(memory_space=pl.ANY)] * len(arrays)
    return pl.pallas_call(
        drain_kernel,
        out_shape=[pltpu.HBM(a.shape, a.dtype) for a in arrays],
        in_specs=anywhere,
        out_specs=anywhere,
        scratch_shapes=[pltpu.SemaphoreType.DMA((len(arrays),))],
        compiler_params=pltpu.CompilerParams(vmem_limit_bytes=2**20),
        name="drain",
    )(*arrays)


def per_device(*arrays):
    return tuple(drain(exchange(*arrays)))


def solution(mesh):
    placed = (
        P(("depth", "col"), "row"),
        P("row", ("depth", "col")),
        P(("depth", "col"), "row"),
        P(("depth", "col"), "row"),
    )
    return jax.shard_map(
        per_device,
        mesh=mesh,
        in_specs=placed,
        out_specs=(
            P(("depth", "col"), "row"),
            P(("depth", "col"), "row"),
            P("row", ("depth", "col")),
            P(("depth", "col"), "row"),
        ),
        check_vma=False,
    )
```

```python
import functools

import jax
import jax.numpy as jnp
from jax import lax
from jax.experimental import pallas as pl
from jax.experimental.pallas import tpu as pltpu
from jax.sharding import PartitionSpec as P

MESH = pl.DeviceIdType.MESH
BF16, F32 = jnp.bfloat16, jnp.float32
OFFSETS = (0, 1, 3, 2)
N_REMOTE = 208
N_LOCAL = 16


def contract_rows(left, right):
    return lax.dot_general(left, right, (((0,), (0,)), ((), ())), preferred_element_type=F32)


def nn(left, right):
    return jnp.dot(left, right, preferred_element_type=F32)


def nt(left, right):
    return lax.dot_general(left, right, (((1,), (1,)), ((), ())), preferred_element_type=F32)


def kernel(
    tokens, w_in, w_out, cotangent,
    out, gin, grad_in, grad_out,
    g_tok, g_cot, e_tok, e_cot, e_act, e_dpre, act_t, wi, wo, pre, dact, s_pre, r_pre, s_dact, r_dact, act, dpre,
    q2, r2, mid, s1, r1, acc, u2, v2, fin, s3, r3,
    send, recv, local,
):
    rows, feat = tokens.shape
    hid = w_in.shape[1]
    slab = 4 * rows
    depth, row, col = lax.axis_index("depth"), lax.axis_index("row"), lax.axis_index("col")
    low = lax.rem(col, 2)
    y = lax.rem(lax.div(col, 2), 4)
    z = lax.div(col, 8)

    def at(dy=0, dz=0, lo=None, r=None, d=None):
        c = lax.rem(z + dz, 4) * 8 + lax.rem(y + dy, 4) * 2 + (low if lo is None else lo)
        return (depth if d is None else d, row if r is None else r, c)

    x_partner = at(lo=1 - low)
    row_partner = at(r=1 - row)
    core_partner = at(d=1 - depth)
    along_y = {o: at(dy=o) for o in (1, 2, 3)}
    along_z = {o: at(dz=o) for o in (1, 2, 3)}
    ring1 = (along_z, along_y)
    ring2 = (along_y, along_z)
    own = (y, z)
    sub = (z, y)

    counter, counter_local, sent, seen = [0], [0], [], set()

    def remote(src, dst, device):
        i = counter[0]
        counter[0] += 1
        copy = pltpu.make_async_remote_copy(
            src_ref=src, dst_ref=dst, send_sem=send.at[i], recv_sem=recv.at[i],
            device_id=device, device_id_type=MESH,
        )
        copy.start()
        sent.append(copy)
        return copy

    def here(src, dst):
        i = counter_local[0]
        counter_local[0] += 1
        copy = pltpu.make_async_copy(src, dst, local.at[i])
        copy.start()
        return copy

    def piece(j):
        return pl.ds(pl.multiple_of(j * rows, rows), rows)

    def ring_at(h, o):
        return lax.rem(own[h] + o, 4)

    my_block = (low, y + low * (z - y), piece(z + low * (y - z)))
    own_copies = [here(tokens, g_tok.at[my_block]), here(cotangent, g_cot.at[my_block])]
    weight_copies = [
        here(w_in, wi.at[:, pl.ds(0, hid)]),
        here(w_out, wo.at[pl.ds(0, hid)]),
    ]

    barrier = pltpu.get_barrier_semaphore()
    friends = [x_partner, row_partner, core_partner] + list(along_y.values()) + list(along_z.values())
    for friend in friends:
        pl.semaphore_signal(barrier, inc=1, device_id=friend, device_id_type=MESH)
    pl.semaphore_wait(barrier, len(friends))

    def arrived(copies):
        for copy in copies:
            if id(copy) not in seen:
                seen.add(id(copy))
                copy.wait_recv()

    def landed(copy):
        if id(copy) not in seen:
            seen.add(id(copy))
            copy.wait()

    def half_of(kind):
        return low if kind == 0 else 1 - low

    def place(kind, di, j):
        h = half_of(kind)
        i0, j0 = y + h * (z - y), z + h * (y - z)
        return h, lax.rem(i0 + di, 4), piece(lax.rem(j0 + j, 4))

    def to_ring1(kind, o):
        h = half_of(kind)
        return at(dy=o * h, dz=o * (1 - h))

    def to_ring2(kind, o):
        h = half_of(kind)
        return at(dy=o * (1 - h), dz=o * h)

    own_src = {0: tokens, 1: cotangent}
    gathered = {0: g_tok, 1: g_cot}
    g0, one, two, three, swapped = {}, {}, {}, {}, {}
    FORWARDS = ((0, 1), (1, 3), (3, 1), (2, 3))

    def send_x(k):
        g0[k] = remote(own_src[k], gathered[k].at[place(0, 0, 0)], x_partner)

    def source(k, kind, block):
        if kind == 0:
            return own_src[k]
        arrived([g0[k]])
        return block

    def columns(k, kind):
        return (0, feat) if k == 0 else (kind * (feat // 2), feat // 2)

    def ring1_send(k, kind):
        block = gathered[k].at[place(kind, 0, 0)]
        src = source(k, kind, block)
        start, size = columns(k, kind)
        cols = pl.ds(start, size)
        one[k, kind] = {
            o: remote(src.at[:, cols], block.at[:, cols], to_ring1(kind, o)) for o in (1, 3)
        }

    def ring1_forward(k, kind):
        for o in (1, 3):
            arrived([one[k, kind][o]])
            h, i, r = place(kind, 0, 4 - o)
            start, size = columns(k, kind)
            block = gathered[k].at[h, i, r, pl.ds(start + (o // 2) * (size // 2), size // 2)]
            one[k, kind, o] = remote(block, block, to_ring1(kind, o))

    def swap(kind, j):
        arrived([one[1, kind, 1], one[1, kind, 3]] if j == 2 else [one[1, kind][4 - j]])
        h, i, r = place(kind, 0, j)
        start, size = columns(1, kind)
        block = g_cot.at[h, i, r, pl.ds(start, size)]
        swapped[kind, j] = remote(block, block, x_partner)

    def ring2_send(k, kind, j):
        block = gathered[k].at[place(kind, 0, j)]
        src = block
        if j == 0:
            src = source(k, kind, block)
        elif j == 2:
            arrived([one[k, kind, 1], one[k, kind, 3]])
        else:
            arrived([one[k, kind][4 - j]])
        if k == 1 and j > 0:
            arrived([swapped[1 - kind, j]])
        two[k, kind, j] = {o: remote(src, block, to_ring2(kind, o)) for o in (1, 3)}

    def forward(k, kind, j, o):
        arrived([two[k, kind, j][o]])
        block = gathered[k].at[place(kind, 4 - o, j)]
        three[k, kind, j, o] = remote(block, block, to_ring2(kind, o))

    def gathered_side(k, o):
        for kind in range(2):
            for j in range(4):
                if (j, o) not in FORWARDS:
                    arrived([two[k, kind, j][o]])

    def gathered_far(k):
        for kind in range(2):
            for j, o in FORWARDS:
                arrived([three[k, kind, j, o]])

    for copy in own_copies:
        landed(copy)

    core, p, q = {}, {}, {}
    mine, other = pl.ds(0, hid), pl.ds(hid, hid)
    tile = feat // 3

    def send_weights():
        core["w_in"] = remote(w_in, wi.at[:, pl.ds(hid, hid)], core_partner)
        core["w_out"] = remote(w_out, wo.at[pl.ds(hid, hid)], core_partner)

    def rows_of(g, o):
        return jnp.concatenate([g[h, ring_at(h, o)] for h in range(2)], axis=0)

    def pre_step(s):
        landed(weight_copies[0])
        arrived([core["w_in"]])
        chunk = rows_of(g_tok, OFFSETS[s])
        p[s] = []
        for part in (mine, other):
            value = nn(chunk, wi[:, part])
            pre[s, :, part] = value
            s_pre[s, :, part] = value.astype(BF16)
            p[s].append(remote(s_pre.at[s, :, part], r_pre.at[s, :, part], row_partner))

    def dact_step(s):
        landed(weight_copies[1])
        arrived([core["w_out"]])
        chunk = rows_of(g_cot, OFFSETS[s])
        q[s] = []
        for part in (mine, other):
            value = nt(chunk, wo[part, :])
            dact[s, :, part] = value
            s_dact[s, :, part] = value.astype(BF16)
            q[s].append(remote(s_dact.at[s, :, part], r_dact.at[s, :, part], row_partner))

    def act_step(s):
        arrived(p[s])
        for h in range(2):
            i = ring_at(h, OFFSETS[s])

            def body(t, _):
                r_in = pl.ds(pl.multiple_of(h * slab + t * 16, 16), 16)
                r_out = pl.ds(pl.multiple_of(t * 16, 16), 16)
                hidden = pre[s, r_in, :] + r_pre[s, r_in, :].astype(F32)
                square = hidden * hidden
                inner = 0.7978845608 * (hidden + 0.044715 * square * hidden)
                tangent = jnp.tanh(inner)
                act[h, i, r_out, :] = (0.5 * hidden * (1.0 + tangent)).astype(BF16)
                pre[s, r_in, :] = 0.5 * (1.0 + tangent) + 0.5 * hidden * (
                    1.0 - tangent * tangent
                ) * 0.7978845608 * (1.0 + 3.0 * 0.044715 * square)
                return 0

            lax.fori_loop(0, slab // 16, body, 0)

    def dpre_step(s):
        arrived(q[s])
        for h in range(2):
            i = ring_at(h, OFFSETS[s])

            def body(t, _):
                r_in = pl.ds(pl.multiple_of(h * slab + t * 16, 16), 16)
                r_out = pl.ds(pl.multiple_of(t * 16, 16), 16)
                total = dact[s, r_in, :] + r_dact[s, r_in, :].astype(F32)
                dpre[h, i, r_out, :] = (total * pre[s, r_in, :]).astype(BF16)
                return 0

            lax.fori_loop(0, slab // 16, body, 0)

    low_rows, high_rows = slice(0, 2 * rows), slice(2 * rows, 4 * rows)

    def span(f):
        return pl.ds(f[0] * (feat // 6), f[1] * (feat // 6))

    def project(k, s, f):
        chunk = rows_of((act, dpre)[k], OFFSETS[s])
        o = OFFSETS[s]
        cols = span(f)
        landed(weight_copies[k - 1])
        arrived([core[("w_out", "w_in")[k]]])
        value = nn(chunk, wo[:, cols]) if k == 0 else nt(chunk, wi[cols, :])
        for h in range(2):
            part = value[h * slab:(h + 1) * slab]
            if o == 2:
                q2[k, h, :, cols] = part.astype(BF16)
            elif o == 1:
                s1[k, h, 0, high_rows, cols] = part[high_rows].astype(BF16)
                mid[k, h, 0, :, cols] = part[low_rows]
            elif o == 3:
                s1[k, h, 1, low_rows, cols] = part[low_rows].astype(BF16)
                mid[k, h, 1, :, cols] = part[high_rows]
            else:
                acc[k, h, :, cols] = part

    whole = (0, 6)
    far, near, merged, second, third = {}, {}, {}, {}, {}

    def scatter_far(k, f):
        far[k, f] = [[] for _ in range(4)]
        for g in ((0, 3), (3, 3)) if k == 0 else (f,):
            project(k, 3, g)
            cols = span(g)
            for h in range(2):
                for side, part in enumerate((low_rows, high_rows)):
                    far[k, f][2 * h + side].append(remote(
                        q2.at[k, h, part, cols], r2.at[k, h, side, :, cols], ring2[h][(1, 3)[side]]
                    ))

    def scatter_near(k, f, side):
        project(k, 1 + side, f)
        part = (high_rows, low_rows)[side]
        cols = span(f)
        near.setdefault((k, f), []).extend(
            remote(s1.at[k, h, side, part, cols], r1.at[k, h, side, part, cols], ring2[h][(1, 3)[side]])
            for h in range(2)
        )

    def scatter_merge(k, f):
        cols = span(f)
        merged[k, f] = []
        for h in range(2):
            for side in range(2):
                arrived(far[k, f][2 * h + side])
                base = side * 2 * rows

                def body(t, _):
                    r_in = pl.ds(pl.multiple_of(t * 16, 16), 16)
                    r_out = pl.ds(pl.multiple_of(base + t * 16, 16), 16)
                    total = mid[k, h, side, r_in, cols] + r2[k, h, side, r_in, cols].astype(F32)
                    s1[k, h, side, r_out, cols] = total.astype(BF16)
                    return 0

                lax.fori_loop(0, 2 * rows // 16, body, 0)
                part = (low_rows, high_rows)[side]
                merged[k, f].append(remote(
                    s1.at[k, h, side, part, cols], r1.at[k, h, side, part, cols],
                    ring2[h][(1, 3)[side]],
                ))

    def scatter_two(k, f):
        cols = span(f)
        arrived(near[k, f])
        arrived(merged[k, f])
        second[k, f] = []
        for h in range(2):
            for slot, o in enumerate((2, 1, 3)):
                r_in = piece(lax.rem(sub[h] + o, 4))
                total = acc[k, h, r_in, cols] + r1[k, h, 0, r_in, cols].astype(F32)
                u2[k, h, slot, :, cols] = (total + r1[k, h, 1, r_in, cols].astype(F32)).astype(BF16)
                second[k, f].append(remote(
                    u2.at[k, h, slot, :, cols], v2.at[k, h, slot, :, cols], ring1[h][o]
                ))

    left_cols, right_cols = pl.ds(0, feat // 2), pl.ds(feat // 2, feat // 2)

    def term(k, h, o, cols):
        r_in = piece(lax.rem(sub[h] + o, 4))
        total = acc[k, h, r_in, cols] + r1[k, h, 0, r_in, cols].astype(F32)
        return total + r1[k, h, 1, r_in, cols].astype(F32)

    def second_send(k, h, slot, cols, o):
        return remote(u2.at[k, h, slot, :, cols], v2.at[k, h, slot, :, cols], ring1[h][o])

    def scatter_two_start(k):
        arrived(near[k, whole])
        arrived(merged[k, whole])
        second[k, whole] = []
        for h in range(2):
            for cols, o in ((left_cols, 1), (right_cols, 3)):
                u2[k, h, 0, :, cols] = term(k, h, 2, cols).astype(BF16)
                second[k, whole].append(second_send(k, h, 0, cols, o))
            u2[k, h, 1, :, right_cols] = term(k, h, 1, right_cols).astype(BF16)
            second[k, whole].append(second_send(k, h, 1, right_cols, 1))
            u2[k, h, 2, :, left_cols] = term(k, h, 3, left_cols).astype(BF16)
            second[k, whole].append(second_send(k, h, 2, left_cols, 3))

    def scatter_two_merge(k):
        for h in range(2):
            for cols, o, slot in ((left_cols, 1, 1), (right_cols, 3, 2)):
                arrived([second[k, whole][4 * h + slot - 1]])
                total = term(k, h, o, cols) + v2[k, h, 0, :, cols].astype(F32)
                u2[k, h, slot, :, cols] = total.astype(BF16)
                second[k, whole].append(second_send(k, h, slot, cols, o))

    def scatter_three(k, f):
        cols = span(f)
        arrived(second[k, f])
        for h in range(2):
            r_in = piece(sub[h])
            total = acc[k, h, r_in, cols] + r1[k, h, 0, r_in, cols].astype(F32)
            total += r1[k, h, 1, r_in, cols].astype(F32)
            for slot in range(1 - k, 3):
                total += v2[k, h, slot, :, cols].astype(F32)
            fin[k, h, :, cols] = total
        s3[k, :, cols] = fin[k, 1 - low, :, cols].astype(BF16)
        third[k, f] = remote(s3.at[k, :, cols], r3.at[k, :, cols], x_partner)

    def finish(k, f):
        cols = span(f)
        arrived([third[k, f]])
        (out, gin)[k][:, cols] = (fin[k, low, :, cols] + r3[k, :, cols].astype(F32)).astype(BF16)

    tokens_all = 8 * slab

    def flat(value):
        return value.reshape(tokens_all, value.shape[-1])

    def send_core(name):
        src, dst = {
            "tok": (g_tok, e_tok),
            "cot": (g_cot, e_cot),
            "act": (act.at[:, :, :, other], e_act),
            "dpre": (dpre.at[:, :, :, other], e_dpre),
        }[name]
        core[name] = remote(src, dst, core_partner)

    def turn_act():
        arrived([core["act"]])
        act_t[0] = jnp.transpose(flat(act[:, :, :, mine]))
        act_t[1] = jnp.transpose(flat(e_act[...]))

    def grad_out_part(start, stop):
        arrived([core["cot"]])

        def body(t, _):
            cols = pl.ds(pl.multiple_of(t * tile, tile), tile)
            value = nn(act_t[0], flat(g_cot[:, :, :, cols]))
            grad_out[:, cols] = value + nn(act_t[1], flat(e_cot[:, :, :, cols]))
            return 0

        lax.fori_loop(start, stop, body, 0)

    def grad_in_part(start, stop):
        arrived([core["tok"], core["dpre"]])

        def body(t, _):
            cols = pl.ds(pl.multiple_of(t * tile, tile), tile)
            value = contract_rows(flat(g_tok[:, :, :, cols]), flat(dpre[:, :, :, mine]))
            value += contract_rows(flat(e_tok[:, :, :, cols]), flat(e_dpre[...]))
            grad_in[cols, :] = value
            return 0

        lax.fori_loop(start, stop, body, 0)

    send_x(0)
    send_weights()
    ring2_send(0, 0, 0)
    ring1_send(1, 0)
    ring1_send(0, 0)
    ring2_send(1, 0, 0)
    send_x(1)
    ring1_forward(1, 0)
    swap(0, 1)
    ring2_send(0, 1, 0)
    swap(0, 3)
    ring1_send(0, 1)
    ring1_forward(0, 0)
    swap(0, 2)
    ring1_send(1, 1)
    ring2_send(1, 1, 0)
    ring2_send(0, 0, 1)
    ring2_send(0, 1, 1)
    ring1_forward(0, 1)
    ring2_send(0, 1, 3)
    swap(1, 1)
    forward(0, 1, 0, 1)
    ring1_forward(1, 1)
    ring2_send(0, 0, 3)
    swap(1, 3)
    forward(0, 0, 0, 1)
    ring2_send(0, 0, 2)
    swap(1, 2)
    ring2_send(0, 1, 2)
    pre_step(0)
    forward(0, 1, 1, 3)
    forward(0, 1, 3, 1)
    forward(0, 0, 1, 3)
    forward(0, 0, 3, 1)
    forward(0, 0, 2, 3)
    forward(0, 1, 2, 3)
    ring2_send(1, 0, 1)
    ring2_send(1, 1, 1)
    ring2_send(1, 0, 3)
    ring2_send(1, 1, 3)
    gathered_side(0, 3)
    ring2_send(1, 1, 2)
    pre_step(1)
    act_step(0)
    gathered_far(0)
    pre_step(3)
    ring2_send(1, 0, 2)
    gathered_side(0, 1)
    forward(1, 0, 0, 1)
    pre_step(2)
    forward(1, 1, 0, 1)
    project(0, 0, whole)
    forward(1, 0, 1, 3)
    forward(1, 1, 1, 3)
    send_core("tok")
    forward(1, 1, 3, 1)
    forward(1, 0, 3, 1)
    forward(1, 0, 2, 3)
    gathered_side(1, 1)
    forward(1, 1, 2, 3)
    act_step(1)
    act_step(3)
    scatter_far(0, whole)
    gathered_side(1, 3)
    dact_step(2)
    gathered_far(1)
    scatter_near(0, whole, 0)
    act_step(2)
    scatter_near(0, whole, 1)
    dact_step(3)
    send_core("cot")
    scatter_merge(0, whole)
    dact_step(1)
    dpre_step(2)
    dact_step(0)
    scatter_near(1, (3, 2), 1)
    dpre_step(3)
    scatter_far(1, (5, 1))
    scatter_far(1, (3, 2))
    scatter_near(1, (5, 1), 1)
    scatter_far(1, (0, 3))
    scatter_two_start(0)
    scatter_near(1, (0, 3), 1)
    dpre_step(1)
    scatter_near(1, (0, 3), 0)
    send_core("act")
    scatter_near(1, (3, 2), 0)
    dpre_step(0)
    scatter_merge(1, (0, 3))
    send_core("dpre")
    scatter_near(1, (5, 1), 0)
    scatter_two_merge(0)
    scatter_merge(1, (3, 2))
    scatter_merge(1, (5, 1))
    turn_act()
    project(1, 0, whole)
    grad_out_part(1, 2)
    scatter_two(1, (0, 3))
    grad_in_part(2, 3)
    scatter_three(0, whole)
    grad_out_part(2, 3)
    scatter_two(1, (3, 2))
    scatter_two(1, (5, 1))
    grad_out_part(0, 1)
    grad_in_part(0, 1)
    scatter_three(1, (0, 3))
    finish(0, whole)
    scatter_three(1, (3, 2))
    scatter_three(1, (5, 1))
    grad_in_part(1, 2)
    finish(1, (0, 3))
    finish(1, (3, 2))
    finish(1, (5, 1))
    for copy in sent:
        copy.wait_send()


def exchange(tokens_in, w_in, w_out, grad_output):
    rows, feat = tokens_in.shape
    hid = w_in.shape[1]
    slab = 4 * rows
    vmem, hbm = pl.BlockSpec(memory_space=pltpu.VMEM), pl.BlockSpec(memory_space=pl.ANY)
    scratch = [
        ((2, 4, slab, feat), BF16),
        ((2, 4, slab, feat), BF16),
        ((2, 4, slab, feat), BF16),
        ((2, 4, slab, feat), BF16),
        ((2, 4, slab, hid), BF16),
        ((2, 4, slab, hid), BF16),
        ((2, hid, 8 * slab), BF16),
        ((feat, 2 * hid), BF16),
        ((2 * hid, feat), BF16),
        ((4, 2 * slab, 2 * hid), F32),
        ((4, 2 * slab, 2 * hid), F32),
        ((4, 2 * slab, 2 * hid), BF16),
        ((4, 2 * slab, 2 * hid), BF16),
        ((4, 2 * slab, 2 * hid), BF16),
        ((4, 2 * slab, 2 * hid), BF16),
        ((2, 4, slab, 2 * hid), BF16),
        ((2, 4, slab, 2 * hid), BF16),
        ((2, 2, slab, feat), BF16),
        ((2, 2, 2, 2 * rows, feat), BF16),
        ((2, 2, 2, 2 * rows, feat), F32),
        ((2, 2, 2, slab, feat), BF16),
        ((2, 2, 2, slab, feat), BF16),
        ((2, 2, slab, feat), F32),
        ((2, 2, 3, rows, feat), BF16),
        ((2, 2, 3, rows, feat), BF16),
        ((2, 2, rows, feat), F32),
        ((2, rows, feat), BF16),
        ((2, rows, feat), BF16),
    ]
    return pl.pallas_call(
        kernel,
        out_shape=[
            pltpu.VMEM((rows, feat), BF16),
            pltpu.VMEM((rows, feat), BF16),
            pltpu.VMEM((feat, hid), F32),
            pltpu.VMEM((hid, feat), F32),
        ],
        in_specs=[hbm] * 4,
        out_specs=[vmem] * 4,
        scratch_shapes=[pltpu.VMEM(*s) for s in scratch] + [
            pltpu.SemaphoreType.DMA((N_REMOTE,)),
            pltpu.SemaphoreType.DMA((N_REMOTE,)),
            pltpu.SemaphoreType.DMA((N_LOCAL,)),
        ],
        compiler_params=pltpu.CompilerParams(
            collective_id=0, has_side_effects=True, vmem_limit_bytes=52 * 2**20
        ),
        name="exchange",
    )(tokens_in, w_in, w_out, grad_output)


def drain_kernel(*refs):
    n = len(refs) // 2
    copies = [pltpu.make_async_copy(refs[i], refs[n + i], refs[-1].at[i]) for i in range(n)]
    for copy in copies:
        copy.start()
    for copy in copies:
        copy.wait()


def drain(arrays):
    arrays = [pltpu.with_memory_space_constraint(a, pltpu.VMEM) for a in arrays]
    anywhere = [pl.BlockSpec(memory_space=pl.ANY)] * len(arrays)
    return pl.pallas_call(
        drain_kernel,
        out_shape=[pltpu.HBM(a.shape, a.dtype) for a in arrays],
        in_specs=anywhere,
        out_specs=anywhere,
        scratch_shapes=[pltpu.SemaphoreType.DMA((len(arrays),))],
        compiler_params=pltpu.CompilerParams(vmem_limit_bytes=2**20),
        name="drain",
    )(*arrays)


def per_device(*arrays):
    return tuple(drain(exchange(*arrays)))


def solution(mesh):
    placed = (
        P(("depth", "col"), "row"),
        P("row", ("depth", "col")),
        P(("depth", "col"), "row"),
        P(("depth", "col"), "row"),
    )
    return jax.shard_map(
        per_device,
        mesh=mesh,
        in_specs=placed,
        out_specs=(
            P(("depth", "col"), "row"),
            P(("depth", "col"), "row"),
            P("row", ("depth", "col")),
            P(("depth", "col"), "row"),
        ),
        check_vma=False,
    )
```
